128 devices in a mesh: leaf: 16 (over x, y), row: 4 (over z_hi, core), col: 2 (over z_lo).
Axes of the slice: x: 4, y: 4, z: 4 (z_hi: 2, z_lo: 2; z = z_hi * 2 + z_lo), core: 2. Of those that a mesh axis runs over, the one named last changes fastest.
Arguments:
- pivot_block: bfloat16 [16, 2048, 2048], P('leaf'), as said below
- coupling: float32 [16, 2048, 2048], P('leaf', ('row', 'col')), may hold values from -0.125 to 0.125, as said below
- parent_front: float32 [4, 16, 128, 8, 8, 128], P(None, 'leaf', None, None, ('row', 'col')), as said below
- child_map: int32 [16, 16], replicated, may hold values from 0 to 63, as said below
Outputs:
- pivot_factor: float32 [16, 2048, 2048], P('leaf', ('row', 'col'))
- child_below: float32 [16, 2048, 2048], P('leaf', ('row', 'col'))
- parent_factor: float32 [4, 16, 128, 8, 8, 128], P(None, 'leaf', None, None, ('row', 'col'))
The draws below stay inside these ranges and needn't reach their ends.
Inputs may be any that keep to these rules, and one draw needn't show every extreme that they name: `pivot_block`: each pivot block is symmetric positive definite. `coupling`: Dense. `parent_front`: Symmetric; after the children's updates are subtracted the front stays positive definite. `child_map`: within a row all 16 entries differ and their residues modulo 16 run once through 0 to 15; each parent block is named by at most 4 children, and some by exactly 4.
All inputs are finite; a program needn't handle non-finite values.
Results may differ from the reference program's by a relative error of at most 0.0004.
Values sent between devices are 32-bit elements; how exact they have to be, the bound alone decides.
No kernel may reach another device: no remote copies, remote signals or barrier semaphores. Data moves between devices by JAX's collectives and lax.ppermute only.
A program may use at most 448 MiB of HBM per device.

```python
import math
import jax
import jax.numpy as jnp
from jax import lax

S = 2048
U = 2048
NP = 8192
BLK = 128
KP = 2
MOST = 4
PANEL = 256
UB = 16
PB = 64
CHILDREN = 16
GROUPS = 8


def sphere_kernel(key, count, length, leading):
    key_height, key_turn = jax.random.split(key)
    height = jax.random.uniform(key_height, leading + (count,), jnp.float32, -1.0, 1.0)
    azimuth = jax.random.uniform(key_turn, leading + (count,), jnp.float32, 0.0, 2.0 * math.pi)
    radius = jnp.sqrt(jnp.maximum(1.0 - height * height, 0.0))
    squared = jnp.zeros(leading + (count, count), jnp.float32)
    for component in (radius * jnp.cos(azimuth), radius * jnp.sin(azimuth), height):
        differ = component[..., :, None] - component[..., None, :]
        squared = squared + differ * differ
    return jnp.exp(-jnp.sqrt(squared) / length)


def with_diagonal(kernel, nugget, count):
    identity = jnp.arange(count)[:, None] == jnp.arange(count)[None, :]
    return kernel + jnp.where(identity, nugget[..., :, None], 0.0)


def draw_pivot_block(key, part):
    key = jax.random.fold_in(key, 11)
    key_points, key_diag = jax.random.split(key)
    length = 9.0 * S ** (-0.5)
    nugget = jax.random.uniform(key_diag, (CHILDREN, S), jnp.float32, 1.0, 2.0)
    kernel = sphere_kernel(key_points, S, length, (CHILDREN,))
    return with_diagonal(kernel, nugget, S).astype(jnp.bfloat16)


def draw_coupling(key, part):
    key = jax.random.fold_in(key, 5)
    key_main = jax.random.fold_in(key, 0)
    spread = ((U + S) // 4) ** (-0.5)
    values = jax.random.truncated_normal(key_main, -4.0, 4.0, (CHILDREN, U, S), jnp.float32)
    return values * spread


def draw_parent_front(key, part):
    key = jax.random.fold_in(key, 23)
    key_points, key_diag = jax.random.split(key)
    length = 9.0 * NP ** (-0.5)
    nugget = jax.random.uniform(key_diag, (NP,), jnp.float32, 90.0, 120.0)
    kernel = 25.0 * sphere_kernel(key_points, NP, length, ())
    matrix = with_diagonal(kernel, nugget, NP)
    return matrix.reshape(PB // CHILDREN, CHILDREN, BLK, PB // GROUPS, GROUPS, BLK)


def shuffled(sub_key, count):
    return jax.random.permutation(sub_key, count)


def draw_child_map(key, part):
    key = jax.random.fold_in(key, 37)
    key_res, key_grp, key_off = jax.random.split(key, 3)
    layers = PB // UB
    residues = jax.vmap(lambda sub_key: shuffled(sub_key, UB))(jax.random.split(key_res, CHILDREN))
    ranks = jax.vmap(lambda sub_key: shuffled(sub_key, CHILDREN))(jax.random.split(key_grp, UB))
    offsets = jax.random.randint(key_off, (UB,), 0, layers)
    levels = (ranks // MOST + offsets[:, None]) % layers
    chosen = levels.T[jnp.arange(CHILDREN)[:, None], residues]
    return (residues + UB * chosen).astype(jnp.int32)


def setup_inputs(seed: int = 0) -> dict:
    key_of = jax.random.split(jax.random.key(seed), 5)
    return {
        "pivot_block": draw_pivot_block(jax.random.fold_in(key_of[4], 71), 0),
        "coupling": draw_coupling(jax.random.fold_in(key_of[4], 71), 0),
        "parent_front": draw_parent_front(jax.random.fold_in(key_of[4], 71), 0),
        "child_map": draw_child_map(jax.random.fold_in(key_of[4], 71), 0),
    }


HIGHEST_PREC = lax.Precision.HIGHEST

def solve_right(factor, rhs_rows):
    return lax.linalg.triangular_solve(factor, rhs_rows, left_side=False, lower=True, transpose_a=True)

def child_front(operands):
    pivot_rows, coupled = operands
    factor = jnp.linalg.cholesky(pivot_rows.astype(jnp.float32))
    return (factor, solve_right(factor, coupled))

def reference(pivot_block, coupling, parent_front, child_map):
    factors, belows = lax.map(child_front, (pivot_block, coupling))
    tiled_front = parent_front.reshape(PB, BLK, PB, BLK)

    def assemble(child_idx, tiled):
        below_rows = belows[child_idx]
        block_ids = child_map[child_idx]
        product = jnp.dot(below_rows.astype(jnp.float32), below_rows.T.astype(jnp.float32), precision=HIGHEST_PREC, preferred_element_type=jnp.float32)
        tile_grid = product.reshape(UB, BLK, UB, BLK).transpose(0, 2, 1, 3)
        return tiled.at[block_ids[:, None], :, block_ids[None, :], :].add(-tile_grid)
    tiled_front = lax.fori_loop(0, CHILDREN, assemble, tiled_front)
    assembled = tiled_front.reshape(NP, NP)
    row_index = jnp.arange(NP, dtype=jnp.int32)
    for panel_idx in range(KP):
        first_col = panel_idx * PANEL
        after_col = first_col + PANEL
        diag_factor = jnp.linalg.cholesky(assembled[first_col:after_col, first_col:after_col])
        solved = solve_right(diag_factor, assembled[:, first_col:after_col])
        trailing = jnp.where((row_index >= after_col)[:, None], solved, 0.0)
        factor_cols = trailing.at[first_col:after_col].set(diag_factor)
        assembled = assembled - jnp.dot(trailing.astype(jnp.float32), trailing.T.astype(jnp.float32), precision=HIGHEST_PREC, preferred_element_type=jnp.float32)
        assembled = assembled.at[:, first_col:after_col].set(factor_cols)
        assembled = assembled.at[first_col:after_col, after_col:].set(0.0)
    parent_factor = assembled.reshape(PB // CHILDREN, CHILDREN, BLK, PB // GROUPS, GROUPS, BLK)
    return (factors, belows, parent_factor)
```

```python
import functools

import jax
import jax.numpy as jnp
from jax import lax
from jax.experimental import pallas as pl
from jax.experimental.pallas import tpu as pltpu
from jax.sharding import PartitionSpec as P

F32 = jnp.float32
BF16 = jnp.bfloat16
S = 2048
BLK = 128
PIVOTS = 512
LEAVES = 16
GROUPS = 8
NB = 256
HB = 128
SUB = 8
STEPS = S // NB
VMEM = pltpu.VMEM
SMEM = pltpu.SMEM
GROUP = ("row", "col")


def dot_t(a, b):
    return lax.dot_general(a, b, (((1,), (1,)), ((), ())), preferred_element_type=F32)


def dot_n(a, b):
    return lax.dot_general(a, b, (((1,), (0,)), ((), ())), preferred_element_type=F32)


def halves(x):
    high = x.astype(BF16)
    low = (x - high.astype(F32)).astype(BF16)
    return high, low


def left3(x, axis=1):
    high, low = halves(x)
    return jnp.concatenate([high, high, low], axis=axis)


def right3(x, axis=1):
    high, low = halves(x)
    return jnp.concatenate([high, low, high], axis=axis)


def mul_t(a, b):
    return dot_t(left3(a), right3(b))


def mul_n(a, b):
    return dot_n(left3(a), right3(b, axis=0))


def eliminate(rows, base):
    sub = lax.broadcasted_iota(jnp.int32, (SUB, HB), 0)
    sub_wide = lax.broadcasted_iota(jnp.int32, rows.shape, 0)
    cols = [jnp.broadcast_to(rows[:, base + j : base + j + 1], (SUB, HB)) for j in range(SUB)]
    for k in range(SUB):
        inv = lax.rsqrt(jnp.broadcast_to(cols[k][k : k + 1, :], (SUB, HB)))
        scaled = cols[k] * inv
        below = jnp.where(sub > k, scaled, 0.0)
        for j in range(k + 1, SUB):
            cols[j] = cols[j] - below * jnp.broadcast_to(scaled[j : j + 1, :], (SUB, HB))
        pivot_row = jnp.broadcast_to(rows[k : k + 1, :], rows.shape) * jnp.concatenate(
            [inv, inv], axis=1
        )
        below_wide = jnp.concatenate([below, below], axis=1)
        rows = jnp.where(sub_wide == k, pivot_row, rows - below_wide * pivot_row)
    return rows


def diag_small(block, work):
    row = lax.broadcasted_iota(jnp.int32, (HB, HB), 0)
    col = lax.broadcasted_iota(jnp.int32, (HB, HB), 1)
    work[:, :HB] = block
    work[:, HB:] = jnp.where(row == col, 1.0, 0.0)
    for base in range(0, HB, SUB):
        rows = eliminate(work[base : base + SUB, :], base)
        work[base : base + SUB, :] = rows
        after = base + SUB
        if after < HB:
            high = rows.astype(BF16).astype(F32)
            low = rows - high
            left = jnp.concatenate([high[:, :HB], high[:, :HB], low[:, :HB]], axis=0).astype(BF16)
            right = jnp.concatenate([high, low, high], axis=0).astype(BF16)
            product = lax.dot_general(
                left, right, (((0,), (0,)), ((), ())), preferred_element_type=F32
            )
            work[after:, :] = work[after:, :] - product[after:, :]
    return jnp.where(col >= row, work[:, :HB], 0.0), work[:, HB:]


def diag_block(block, work):
    upper_a, inv_a = diag_small(block[:HB, :HB], work)
    low_left = mul_t(block[HB:, :HB], inv_a)
    upper_b, inv_b = diag_small(block[HB:, HB:] - mul_t(low_left, low_left), work)
    inv_low = -mul_n(inv_b, mul_n(low_left, inv_a))
    zero = jnp.zeros((HB, HB), F32)
    factor = jnp.concatenate(
        [
            jnp.concatenate([upper_a.T, zero], axis=1),
            jnp.concatenate([low_left, upper_b.T], axis=1),
        ],
        axis=0,
    )
    inverse = jnp.concatenate(
        [
            jnp.concatenate([inv_a, zero], axis=1),
            jnp.concatenate([inv_low, inv_b], axis=1),
        ],
        axis=0,
    )
    return factor, inverse


def part(i):
    return pl.ds(pl.multiple_of(i * NB, NB), NB)


def factor_kernel(p_ref, c_ref, l_ref, b_ref, inv_ref, work, left, right):
    def load_row(i, _):
        def load(k, _):
            l_ref[part(i), part(k)] = p_ref[part(i), part(k)].astype(F32)
            return 0

        def clear(k, _):
            l_ref[part(i), part(k)] = jnp.zeros((NB, NB), F32)
            return 0

        lax.fori_loop(0, i + 1, load, 0)
        lax.fori_loop(i + 1, STEPS, clear, 0)
        return 0

    lax.fori_loop(0, STEPS, load_row, 0)
    b_ref[...] = c_ref[...]

    def step(j, _):
        factor, inverse = diag_block(l_ref[part(j), part(j)], work)
        l_ref[part(j), part(j)] = factor
        inv_ref[j] = inverse
        inverse_parts = right3(inverse)
        own = dot_t(left3(b_ref[:, part(j)]), inverse_parts)
        b_ref[:, part(j)] = own
        own_parts = left3(own)

        def panel(i, _):
            x = dot_t(left3(l_ref[part(i), part(j)]), inverse_parts)
            l_ref[part(i), part(j)] = x
            left[part(i), :] = left3(x)
            right[part(i), :] = right3(x)
            return 0

        lax.fori_loop(j + 1, STEPS, panel, 0)

        def trail(k, _):
            b_ref[:, part(k)] = b_ref[:, part(k)] - dot_t(own_parts, right[part(k), :])

            def trail_row(i, _):
                l_ref[part(i), part(k)] = l_ref[part(i), part(k)] - dot_t(
                    left[part(i), :], right[part(k), :]
                )
                return 0

            lax.fori_loop(k, STEPS, trail_row, 0)
            return 0

        lax.fori_loop(j + 1, STEPS, trail, 0)
        return 0

    lax.fori_loop(0, STEPS, step, 0)


def factor_child(pivot, coupling):
    return pl.pallas_call(
        factor_kernel,
        out_shape=(
            jax.ShapeDtypeStruct((S, S), F32),
            jax.ShapeDtypeStruct((NB, S), F32),
            jax.ShapeDtypeStruct((STEPS, NB, NB), F32),
        ),
        in_specs=[pl.BlockSpec(memory_space=VMEM)] * 2,
        out_specs=(pl.BlockSpec(memory_space=VMEM),) * 3,
        scratch_shapes=[
            VMEM((HB, 2 * HB), F32),
            VMEM((S, 3 * NB), BF16),
            VMEM((S, 3 * NB), BF16),
        ],
        compiler_params=pltpu.CompilerParams(vmem_limit_bytes=56 * 2**20),
        cost_estimate=pl.CostEstimate(
            flops=150 * 10**9, bytes_accessed=30 * 2**20, transcendentals=0
        ),
    )(pivot, coupling)


SOLVED = 3


def solve_kernel(l_hbm, inv_ref, *refs):
    ins = refs[:SOLVED]
    outs = refs[SOLVED : 2 * SOLVED]
    l_vmem, c_vmem, high, low, sems = refs[2 * SOLVED :]

    def l_copy(j):
        where = (pl.ds(j * NB, NB), pl.ds(0, (j + 1) * NB))
        return pltpu.make_async_copy(l_hbm.at[where], l_vmem.at[where], sems.at[j])

    def c_copy(j, i):
        cols = pl.ds(j * NB, NB)
        return pltpu.make_async_copy(
            ins[i].at[:, cols], c_vmem.at[pl.ds(i * NB, NB), cols], sems.at[STEPS + j * SOLVED + i]
        )

    for j in range(STEPS):
        l_copy(j).start()
        for i in range(SOLVED):
            c_copy(j, i).start()
    for j in range(STEPS):
        l_copy(j).wait()
        for i in range(SOLVED):
            c_copy(j, i).wait()
        rhs = c_vmem[:, j * NB : (j + 1) * NB]
        if j:
            before = slice(0, j * NB)
            f_high, f_low = halves(l_vmem[j * NB : (j + 1) * NB, before])
            rhs = rhs - (
                dot_t(high[:, before], f_high)
                + dot_t(high[:, before], f_low)
                + dot_t(low[:, before], f_high)
            )
        x = mul_t(rhs, inv_ref[j])
        x_high, x_low = halves(x)
        high[:, j * NB : (j + 1) * NB] = x_high
        low[:, j * NB : (j + 1) * NB] = x_low
        for i in range(SOLVED):
            outs[i][:, j * NB : (j + 1) * NB] = x[i * NB : (i + 1) * NB]


def solve_rows(factor, inverses, rows):
    return pl.pallas_call(
        solve_kernel,
        out_shape=(jax.ShapeDtypeStruct((NB, S), F32),) * SOLVED,
        in_specs=[pl.BlockSpec(memory_space=pl.ANY), pl.BlockSpec(memory_space=VMEM)]
        + [pl.BlockSpec(memory_space=pl.ANY)] * SOLVED,
        out_specs=(pl.BlockSpec(memory_space=VMEM),) * SOLVED,
        scratch_shapes=[
            VMEM((S, S), F32),
            VMEM((SOLVED * NB, S), F32),
            VMEM((SOLVED * NB, S), BF16),
            VMEM((SOLVED * NB, S), BF16),
            pltpu.SemaphoreType.DMA((STEPS * (1 + SOLVED),)),
        ],
        compiler_params=pltpu.CompilerParams(vmem_limit_bytes=56 * 2**20),
        cost_estimate=pl.CostEstimate(
            flops=20 * 10**9, bytes_accessed=24 * 2**20, transcendentals=0
        ),
    )(factor, inverses, *rows)


def update_kernel(place, map_ref, *refs):
    ins = refs[:GROUPS]
    out, tiles, chosen, high, low, sems = refs[GROUPS:]
    leaf = place[0]
    group = place[1]
    for s in range(GROUPS):
        for half in range(2):
            tile = (group ^ s) * 2 + half
            dest = lax.rem(map_ref[leaf, tile], LEAVES)
            rows = pl.ds(half * BLK, BLK)
            pltpu.make_async_copy(ins[s].at[rows, :], tiles.at[dest], sems.at[dest]).start()
            for pick in range(2):

                @pl.when(dest == group + pick * GROUPS)
                def _():
                    pltpu.make_async_copy(
                        ins[s].at[rows, :],
                        chosen.at[pl.ds(pick * BLK, BLK), :],
                        sems.at[LEAVES + pick],
                    ).start()

    for pick in range(2):
        pltpu.make_async_copy(
            ins[0].at[pl.ds(0, BLK), :],
            chosen.at[pl.ds(pick * BLK, BLK), :],
            sems.at[LEAVES + pick],
        ).wait()
    high[...], low[...] = halves(chosen[...])
    together = 4

    def tile_group(q, _):
        for t in range(together):
            pltpu.make_async_copy(
                ins[0].at[pl.ds(0, BLK), :],
                tiles.at[q * together + t],
                sems.at[q * together + t],
            ).wait()
        rows = tiles[pl.ds(q * together, together)].reshape(together * BLK, S)
        r_high, r_low = halves(rows)
        product = (
            dot_t(r_high, high[...]) + dot_t(r_high, low[...]) + dot_t(r_low, high[...])
        )
        for t in range(together):
            for pick in range(2):
                out[q * together + t, pick] = product[
                    t * BLK : (t + 1) * BLK, pick * BLK : (pick + 1) * BLK
                ]
        return 0

    lax.fori_loop(0, LEAVES // together, tile_group, 0)


def update_blocks(place, child_map, rows):
    return pl.pallas_call(
        update_kernel,
        out_shape=jax.ShapeDtypeStruct((LEAVES, 2, BLK, BLK), F32),
        in_specs=[pl.BlockSpec(memory_space=SMEM)] * 2
        + [pl.BlockSpec(memory_space=pl.ANY)] * GROUPS,
        out_specs=pl.BlockSpec(memory_space=VMEM),
        scratch_shapes=[
            VMEM((LEAVES, BLK, S), F32),
            VMEM((2 * BLK, S), F32),
            VMEM((2 * BLK, S), BF16),
            VMEM((2 * BLK, S), BF16),
            pltpu.SemaphoreType.DMA((LEAVES + 2,)),
        ],
        compiler_params=pltpu.CompilerParams(vmem_limit_bytes=56 * 2**20),
        cost_estimate=pl.CostEstimate(
            flops=8 * 10**9, bytes_accessed=20 * 2**20, transcendentals=0
        ),
    )(place, child_map, *rows)


def assemble_kernel(place, map_ref, got, parent, front, row_level, col_slot):
    leaf = place[0]
    group = place[1]

    def find(c, _):
        level = jnp.int32(0)
        slots = [jnp.int32(0), jnp.int32(0)]
        for t in range(LEAVES):
            block = map_ref[c, t]
            residue = block & (LEAVES - 1)
            level = jnp.where(residue == leaf, block >> 4, level)
            for pick in range(2):
                slots[pick] = jnp.where(
                    residue == group + pick * GROUPS, block >> 3, slots[pick]
                )
        row_level[c] = level
        for pick in range(2):
            col_slot[c, pick] = slots[pick]
        return 0

    lax.fori_loop(0, LEAVES, find, 0)
    for k in range(8):
        front[k] = parent[pl.ds(k, 4 * BLK, 8), :]

    def subtract(c, _):
        rows = pl.ds(pl.multiple_of(row_level[c] * BLK, BLK), BLK)
        for pick in range(2):
            slot = col_slot[c, pick]
            front[slot, rows, :] = front[slot, rows, :] - got[c, pick]
        return 0

    lax.fori_loop(0, LEAVES, subtract, 0)


def assemble(place, child_map, got, parent):
    return pl.pallas_call(
        assemble_kernel,
        out_shape=jax.ShapeDtypeStruct((8, 4 * BLK, BLK), F32),
        in_specs=[pl.BlockSpec(memory_space=SMEM)] * 2 + [pl.BlockSpec(memory_space=VMEM)] * 2,
        out_specs=pl.BlockSpec(memory_space=VMEM),
        scratch_shapes=[SMEM((LEAVES,), jnp.int32), SMEM((LEAVES, 2), jnp.int32)],
        compiler_params=pltpu.CompilerParams(vmem_limit_bytes=32 * 2**20),
        cost_estimate=pl.CostEstimate(
            flops=10**6, bytes_accessed=6 * 2**20, transcendentals=0
        ),
    )(place, child_map, got, parent)


def panel_kernel(place, d0, d1, d2, d3, l_ref, inv_ref, block, work):
    group = place[1]
    for i, ref in enumerate((d0, d1, d2, d3)):
        block[(group & 3) ^ i] = ref[...]

    def square(r, c):
        rows = slice(r * NB, (r + 1) * NB)
        return jnp.concatenate([block[2 * c, rows, :], block[2 * c + 1, rows, :]], axis=1)

    factor_a, inv_a = diag_block(square(0, 0), work)
    low_left = mul_t(square(1, 0), inv_a)
    factor_b, inv_b = diag_block(square(1, 1) - mul_t(low_left, low_left), work)
    zero = jnp.zeros((NB, NB), F32)
    l_ref[:NB, :NB] = factor_a
    l_ref[:NB, NB:] = zero
    l_ref[NB:, :NB] = low_left
    l_ref[NB:, NB:] = factor_b
    inv_ref[:NB, :NB] = inv_a
    inv_ref[:NB, NB:] = zero
    inv_ref[NB:, :NB] = -mul_n(inv_b, mul_n(low_left, inv_a))
    inv_ref[NB:, NB:] = inv_b


def factor_panel(place, columns):
    return pl.pallas_call(
        panel_kernel,
        out_shape=(jax.ShapeDtypeStruct((PIVOTS, PIVOTS), F32),) * 2,
        in_specs=[pl.BlockSpec(memory_space=SMEM)] + [pl.BlockSpec(memory_space=VMEM)] * 4,
        out_specs=(pl.BlockSpec(memory_space=VMEM),) * 2,
        scratch_shapes=[VMEM((4, PIVOTS, BLK), F32), VMEM((HB, 2 * HB), F32)],
        compiler_params=pltpu.CompilerParams(vmem_limit_bytes=32 * 2**20),
        cost_estimate=pl.CostEstimate(
            flops=25 * 10**9, bytes_accessed=4 * 2**20, transcendentals=0
        ),
    )(place, *columns)


def trailing_kernel(
    place, front, x0, x1, x2, x3, y0, y1, y2, y3, l_ref, inv_ref, out, panel, above
):
    leaf = place[0]
    group = place[1]
    for i, ref in enumerate((x0, x1, x2, x3)):
        panel[(group & 3) ^ i] = ref[...]
    for i, ref in enumerate((y0, y1, y2, y3)):
        above[(leaf - i) & 3] = ref[...]
    inverse = inv_ref[...]
    own = jnp.concatenate([panel[i] for i in range(4)], axis=1)
    solved = mul_t(own, inverse)
    solved_parts = left3(solved)
    inverse_parts = left3(inverse)
    row = lax.broadcasted_iota(jnp.int32, (PIVOTS, BLK), 0)
    in_panel = (row < BLK) & (leaf < 4)
    for pair in range(4):
        across = jnp.concatenate(
            [
                jnp.concatenate([above[q, 2 * pair], above[q, 2 * pair + 1]], axis=1)
                for q in range(4)
            ],
            axis=0,
        )
        across = dot_n(inverse_parts, right3(across, axis=0))
        change = dot_n(solved_parts, right3(across, axis=0))
        for half in range(2):
            k = 2 * pair + half
            value = front[k] - change[:, half * BLK : (half + 1) * BLK]
            out[pl.ds(k, PIVOTS, 8), :] = jnp.where(in_panel, 0.0, value)

    for i in range(4):

        @pl.when(group == i)
        def _():
            out[pl.ds(0, PIVOTS, 8), :] = solved[:, i * BLK : (i + 1) * BLK]

            @pl.when(leaf < 4)
            def _():
                rows = pl.ds(pl.multiple_of((leaf & 3) * BLK, BLK), BLK)
                out[pl.ds(0, BLK, 8), :] = l_ref[rows, i * BLK : (i + 1) * BLK]


def finish(place, front, columns, rows, factor, inverse):
    return pl.pallas_call(
        trailing_kernel,
        out_shape=jax.ShapeDtypeStruct((8 * PIVOTS, BLK), F32),
        in_specs=[pl.BlockSpec(memory_space=SMEM)] + [pl.BlockSpec(memory_space=VMEM)] * 11,
        out_specs=pl.BlockSpec(memory_space=VMEM),
        scratch_shapes=[VMEM((4, PIVOTS, BLK), F32), VMEM((4, 8, BLK, BLK), F32)],
        compiler_params=pltpu.CompilerParams(vmem_limit_bytes=48 * 2**20),
        cost_estimate=pl.CostEstimate(
            flops=5 * 10**9, bytes_accessed=12 * 2**20, transcendentals=0
        ),
    )(place, front, *columns, *rows, factor, inverse)


def group_swap(x, mask, sources=GROUPS):
    return lax.ppermute(x, GROUP, [(a, a ^ mask) for a in range(sources)])


def leaf_column(x, leaf):
    sent = [lax.ppermute(x, "leaf", [(y, 4 * to + y) for y in range(4)]) for to in (1, 2, 3)]
    return jnp.where(leaf < 4, x, sent[0] + sent[1] + sent[2])


def leaf_row(x):
    turned = [
        lax.ppermute(x, "leaf", [(a, (a & 12) | ((a + by) & 3)) for a in range(LEAVES)])
        for by in (1, 2, 3)
    ]
    return [x] + turned


def panel_columns(x, group):
    near = group_swap(x, 1, 4)
    far = group_swap(x, 4, 4)
    across = group_swap(x, 5, 4)
    mine = group < 4
    first = jnp.where(mine, x, far)
    second = jnp.where(mine, near, across)
    return [first, second, group_swap(first, 2), group_swap(second, 2)]


def local(pivot_block, coupling, parent_front, child_map):
    leaf = lax.axis_index("leaf")
    group = lax.axis_index(GROUP)
    place = jnp.stack([leaf, group]).astype(jnp.int32)
    coupled = coupling[0]
    others = [group_swap(coupled, mask) for mask in (1, 5, 4)]
    factor, below, inverses = factor_child(pivot_block[0], coupled)
    below_near, below_across, below_far = solve_rows(factor, inverses, others)
    have = {0: below, 1: below_near, 5: below_across, 4: below_far}
    have.update({mask ^ 2: group_swap(x, 2) for mask, x in list(have.items())})
    products = update_blocks(place, child_map, [have[s] for s in range(GROUPS)])
    got = lax.all_to_all(products, "leaf", split_axis=0, concat_axis=0, tiled=True)
    front = assemble(place, child_map, got, parent_front.reshape(8 * PIVOTS, BLK))
    diag_rows = leaf_row(leaf_column(front[0, :BLK], leaf))
    turn = [diag_rows[i] for i in range(4)]
    spot = leaf & 3
    ordered = jnp.stack(turn)[(spot - jnp.arange(4)) & 3].reshape(PIVOTS, BLK)
    panel_factor, panel_inverse = factor_panel(place, panel_columns(ordered, group))
    columns = panel_columns(front[0], group)
    rows = leaf_row(leaf_column(front[:, :BLK], leaf))
    result = finish(place, front, columns, rows, panel_factor, panel_inverse)
    factor_own = lax.dynamic_slice_in_dim(factor, group * NB, NB, 0)
    return (
        factor_own[None],
        below[None],
        result.reshape(4, 1, BLK, 8, 1, BLK),
    )


def solution(mesh):
    return jax.shard_map(
        local,
        mesh=mesh,
        in_specs=(
            P("leaf", None, None),
            P("leaf", GROUP, None),
            P(None, "leaf", None, None, GROUP, None),
            P(),
        ),
        out_specs=(
            P("leaf", GROUP, None),
            P("leaf", GROUP, None),
            P(None, "leaf", None, None, GROUP, None),
        ),
        check_vma=False,
    )
```

```python
import functools

import jax
import jax.numpy as jnp
from jax import lax
from jax.experimental import pallas as pl
from jax.experimental.pallas import tpu as pltpu
from jax.sharding import PartitionSpec as P

F32 = jnp.float32
BF16 = jnp.bfloat16
S = 2048
BLK = 128
PIVOTS = 512
LEAVES = 16
GROUPS = 8
NB = 256
HB = 128
PIECE = 32
SUB = 32
STEPS = S // NB
VMEM = pltpu.VMEM
SMEM = pltpu.SMEM
GROUP = ("row", "col")


def dot_t(a, b):
    return lax.dot_general(a, b, (((1,), (1,)), ((), ())), preferred_element_type=F32)


def dot_n(a, b):
    return lax.dot_general(a, b, (((1,), (0,)), ((), ())), preferred_element_type=F32)


def halves(x):
    high = x.astype(BF16)
    low = (x - high.astype(F32)).astype(BF16)
    return high, low


def left3(x, axis=1):
    high, low = halves(x)
    return jnp.concatenate([high, high, low], axis=axis)


def right3(x, axis=1):
    high, low = halves(x)
    return jnp.concatenate([high, low, high], axis=axis)


def mul_t(a, b):
    return dot_t(left3(a), right3(b))


def mul_n(a, b):
    return dot_n(left3(a), right3(b, axis=0))


def eliminate(rows, base):
    groups = SUB // 8
    sub = lax.broadcasted_iota(jnp.int32, (8, HB), 0)
    state = [
        [rows[8 * a : 8 * a + 8, HB * h : HB * h + HB] for h in range(2)] for a in range(groups)
    ]
    cols = [
        [
            jnp.broadcast_to(rows[8 * a : 8 * a + 8, base + j : base + j + 1], (8, HB))
            if a >= j // 8
            else None
            for a in range(groups)
        ]
        for j in range(SUB)
    ]
    for k in range(SUB):
        own, line = divmod(k, 8)
        inv = lax.rsqrt(jnp.broadcast_to(cols[k][own][line : line + 1, :], (8, HB)))
        scaled = [cols[k][a] * inv if a >= own else None for a in range(groups)]
        below = list(scaled)
        below[own] = jnp.where(sub > line, scaled[own], 0.0)
        for j in range(k + 1, SUB):
            at, spot = divmod(j, 8)
            across = jnp.broadcast_to(scaled[at][spot : spot + 1, :], (8, HB))
            for a in range(at, groups):
                cols[j][a] = cols[j][a] - below[a] * across
        for h in range(2):
            pivot_row = jnp.broadcast_to(state[own][h][line : line + 1, :], (8, HB)) * inv
            state[own][h] = jnp.where(
                sub == line, pivot_row, state[own][h] - below[own] * pivot_row
            )
            for a in range(own + 1, groups):
                state[a][h] = state[a][h] - below[a] * pivot_row
    return jnp.concatenate([jnp.concatenate(pair, axis=1) for pair in state], axis=0)


def diag_small(block, work):
    row = lax.broadcasted_iota(jnp.int32, (HB, HB), 0)
    col = lax.broadcasted_iota(jnp.int32, (HB, HB), 1)
    work[:, :HB] = block
    work[:, HB:] = jnp.where(row == col, 1.0, 0.0)
    for base in range(0, HB, SUB):
        rows = eliminate(work[base : base + SUB, :], base)
        work[base : base + SUB, :] = rows
        after = base + SUB
        if after < HB:
            high = rows.astype(BF16).astype(F32)
            low = rows - high
            left = jnp.concatenate([high[:, :HB], high[:, :HB], low[:, :HB]], axis=0).astype(BF16)
            right = jnp.concatenate([high, low, high], axis=0).astype(BF16)
            product = lax.dot_general(
                left, right, (((0,), (0,)), ((), ())), preferred_element_type=F32
            )
            work[after:, :] = work[after:, :] - product[after:, :]
    return jnp.where(col >= row, work[:, :HB], 0.0), work[:, HB:]


def diag_block(block, work):
    upper_a, inv_a = diag_small(block[:HB, :HB], work)
    low_left = mul_t(block[HB:, :HB], inv_a)
    upper_b, inv_b = diag_small(block[HB:, HB:] - mul_t(low_left, low_left), work)
    inv_low = -mul_n(inv_b, mul_n(low_left, inv_a))
    zero = jnp.zeros((HB, HB), F32)
    factor = jnp.concatenate(
        [
            jnp.concatenate([upper_a.T, zero], axis=1),
            jnp.concatenate([low_left, upper_b.T], axis=1),
        ],
        axis=0,
    )
    inverse = jnp.concatenate(
        [
            jnp.concatenate([inv_a, zero], axis=1),
            jnp.concatenate([inv_low, inv_b], axis=1),
        ],
        axis=0,
    )
    return factor, inverse


def part(i):
    return pl.ds(pl.multiple_of(i * NB, NB), NB)


def factor_kernel(p_ref, c_ref, l_ref, b_ref, inv_ref, work, left, right):
    def load_row(i, _):
        def load(k, _):
            l_ref[part(i), part(k)] = p_ref[part(i), part(k)].astype(F32)
            return 0

        def clear(k, _):
            l_ref[part(i), part(k)] = jnp.zeros((NB, NB), F32)
            return 0

        lax.fori_loop(0, i + 1, load, 0)
        lax.fori_loop(i + 1, STEPS, clear, 0)
        return 0

    lax.fori_loop(0, STEPS, load_row, 0)
    b_ref[...] = c_ref[...]

    def step(j, _):
        factor, inverse = diag_block(l_ref[part(j), part(j)], work)
        l_ref[part(j), part(j)] = factor
        inv_ref[j] = inverse
        inverse_parts = right3(inverse)
        own = dot_t(left3(b_ref[:, part(j)]), inverse_parts)
        b_ref[:, part(j)] = own
        own_parts = left3(own)

        def panel(i, _):
            x = dot_t(left3(l_ref[part(i), part(j)]), inverse_parts)
            l_ref[part(i), part(j)] = x
            left[part(i), :] = left3(x)
            right[part(i), :] = right3(x)
            return 0

        lax.fori_loop(j + 1, STEPS, panel, 0)

        def trail(k, _):
            b_ref[:, part(k)] = b_ref[:, part(k)] - dot_t(own_parts, right[part(k), :])

            def trail_row(i, _):
                l_ref[part(i), part(k)] = l_ref[part(i), part(k)] - dot_t(
                    left[part(i), :], right[part(k), :]
                )
                return 0

            lax.fori_loop(k, STEPS, trail_row, 0)
            return 0

        lax.fori_loop(j + 1, STEPS, trail, 0)
        return 0

    lax.fori_loop(0, STEPS, step, 0)


def factor_child(pivot, coupling):
    return pl.pallas_call(
        factor_kernel,
        out_shape=(
            jax.ShapeDtypeStruct((S, S), F32),
            jax.ShapeDtypeStruct((NB, S), F32),
            jax.ShapeDtypeStruct((STEPS, NB, NB), F32),
        ),
        in_specs=[pl.BlockSpec(memory_space=VMEM)] * 2,
        out_specs=(pl.BlockSpec(memory_space=VMEM),) * 3,
        scratch_shapes=[
            VMEM((HB, 2 * HB), F32),
            VMEM((S, 3 * NB), BF16),
            VMEM((S, 3 * NB), BF16),
        ],
        compiler_params=pltpu.CompilerParams(vmem_limit_bytes=56 * 2**20),
        cost_estimate=pl.CostEstimate(
            flops=150 * 10**9, bytes_accessed=30 * 2**20, transcendentals=0
        ),
    )(pivot, coupling)


SOLVED = 3


def solve_kernel(l_hbm, inv_ref, *refs):
    ins = refs[:SOLVED]
    outs = refs[SOLVED : 2 * SOLVED]
    l_vmem, c_vmem, high, low, sems = refs[2 * SOLVED :]

    def l_copy(j):
        where = (pl.ds(j * NB, NB), pl.ds(0, (j + 1) * NB))
        return pltpu.make_async_copy(l_hbm.at[where], l_vmem.at[where], sems.at[j])

    def c_copy(j, i):
        cols = pl.ds(j * NB, NB)
        return pltpu.make_async_copy(
            ins[i].at[:, cols], c_vmem.at[pl.ds(i * NB, NB), cols], sems.at[STEPS + j * SOLVED + i]
        )

    for j in range(STEPS):
        l_copy(j).start()
        for i in range(SOLVED):
            c_copy(j, i).start()
    for j in range(STEPS):
        l_copy(j).wait()
        for i in range(SOLVED):
            c_copy(j, i).wait()
        rhs = c_vmem[:, j * NB : (j + 1) * NB]
        if j:
            before = slice(0, j * NB)
            f_high, f_low = halves(l_vmem[j * NB : (j + 1) * NB, before])
            rhs = rhs - (
                dot_t(high[:, before], f_high)
                + dot_t(high[:, before], f_low)
                + dot_t(low[:, before], f_high)
            )
        x = mul_t(rhs, inv_ref[j])
        x_high, x_low = halves(x)
        high[:, j * NB : (j + 1) * NB] = x_high
        low[:, j * NB : (j + 1) * NB] = x_low
        for i in range(SOLVED):
            outs[i][:, j * NB : (j + 1) * NB] = x[i * NB : (i + 1) * NB]


def solve_rows(factor, inverses, rows):
    return pl.pallas_call(
        solve_kernel,
        out_shape=(jax.ShapeDtypeStruct((NB, S), F32),) * SOLVED,
        in_specs=[pl.BlockSpec(memory_space=pl.ANY), pl.BlockSpec(memory_space=VMEM)]
        + [pl.BlockSpec(memory_space=pl.ANY)] * SOLVED,
        out_specs=(pl.BlockSpec(memory_space=VMEM),) * SOLVED,
        scratch_shapes=[
            VMEM((S, S), F32),
            VMEM((SOLVED * NB, S), F32),
            VMEM((SOLVED * NB, S), BF16),
            VMEM((SOLVED * NB, S), BF16),
            pltpu.SemaphoreType.DMA((STEPS * (1 + SOLVED),)),
        ],
        compiler_params=pltpu.CompilerParams(vmem_limit_bytes=56 * 2**20),
        cost_estimate=pl.CostEstimate(
            flops=20 * 10**9, bytes_accessed=24 * 2**20, transcendentals=0
        ),
    )(factor, inverses, *rows)


def update_kernel(place, map_ref, *refs):
    ins = refs[:GROUPS]
    out, tiles, chosen, high, low, sems = refs[GROUPS:]
    leaf = place[0]
    group = place[1]
    for s in range(GROUPS):
        for half in range(2):
            tile = (group ^ s) * 2 + half
            dest = lax.rem(map_ref[leaf, tile], LEAVES)
            rows = pl.ds(half * BLK, BLK)
            pltpu.make_async_copy(ins[s].at[rows, :], tiles.at[dest], sems.at[dest]).start()
            for pick in range(2):

                @pl.when(dest == group + pick * GROUPS)
                def _():
                    pltpu.make_async_copy(
                        ins[s].at[rows, :],
                        chosen.at[pl.ds(pick * BLK, BLK), :],
                        sems.at[LEAVES + pick],
                    ).start()

    for pick in range(2):
        pltpu.make_async_copy(
            ins[0].at[pl.ds(0, BLK), :],
            chosen.at[pl.ds(pick * BLK, BLK), :],
            sems.at[LEAVES + pick],
        ).wait()
    high[...], low[...] = halves(chosen[...])
    together = 4

    def tile_group(q, _):
        for t in range(together):
            pltpu.make_async_copy(
                ins[0].at[pl.ds(0, BLK), :],
                tiles.at[q * together + t],
                sems.at[q * together + t],
            ).wait()
        rows = tiles[pl.ds(q * together, together)].reshape(together * BLK, S)
        r_high, r_low = halves(rows)
        product = (
            dot_t(r_high, high[...]) + dot_t(r_high, low[...]) + dot_t(r_low, high[...])
        )
        for t in range(together):
            for pick in range(2):
                out[q * together + t, pick * BLK : (pick + 1) * BLK] = product[
                    t * BLK : (t + 1) * BLK, pick * BLK : (pick + 1) * BLK
                ]

        @pl.when(q == 0)
        def _():
            for y in range(together):
                level = jnp.int32(0)
                for t in range(LEAVES):
                    block = map_ref[leaf, t]
                    level = jnp.where((block & (LEAVES - 1)) == y, block >> 4, level)
                keep = jnp.where(level == 0, 1.0, 0.0).astype(F32)
                for x in range(4):
                    for pick in range(2):
                        start = 2 * BLK + pick * PIECE
                        out[4 * x + y, start : start + PIECE] = keep * product[
                            y * BLK + x * PIECE : y * BLK + (x + 1) * PIECE,
                            pick * BLK : (pick + 1) * BLK,
                        ]

        return 0

    lax.fori_loop(0, LEAVES // together, tile_group, 0)


def update_blocks(place, child_map, rows):
    return pl.pallas_call(
        update_kernel,
        out_shape=jax.ShapeDtypeStruct((LEAVES, 2 * (BLK + PIECE), BLK), F32),
        in_specs=[pl.BlockSpec(memory_space=SMEM)] * 2
        + [pl.BlockSpec(memory_space=pl.ANY)] * GROUPS,
        out_specs=pl.BlockSpec(memory_space=VMEM),
        scratch_shapes=[
            VMEM((LEAVES, BLK, S), F32),
            VMEM((2 * BLK, S), F32),
            VMEM((2 * BLK, S), BF16),
            VMEM((2 * BLK, S), BF16),
            pltpu.SemaphoreType.DMA((LEAVES + 2,)),
        ],
        compiler_params=pltpu.CompilerParams(vmem_limit_bytes=56 * 2**20),
        cost_estimate=pl.CostEstimate(
            flops=8 * 10**9, bytes_accessed=20 * 2**20, transcendentals=0
        ),
    )(place, child_map, *rows)


def assemble_kernel(
    place, map_ref, got, parent, p1, p2, p3, front, piece, spread, row_level, col_slot
):
    leaf = place[0]
    group = place[1]

    def find(c, _):
        level = jnp.int32(0)
        slots = [jnp.int32(0), jnp.int32(0)]
        for t in range(LEAVES):
            block = map_ref[c, t]
            residue = block & (LEAVES - 1)
            level = jnp.where(residue == leaf, block >> 4, level)
            for pick in range(2):
                slots[pick] = jnp.where(
                    residue == group + pick * GROUPS, block >> 3, slots[pick]
                )
        row_level[c] = level
        for pick in range(2):
            col_slot[c, pick] = slots[pick]
        return 0

    lax.fori_loop(0, LEAVES, find, 0)
    mine = leaf < 4
    for k in range(8):
        front[k] = parent[pl.ds(k, 4 * BLK, 8), :]
        rows = pl.ds(k, PIECE, 8)
        sent = p1[rows, :] + p2[rows, :] + p3[rows, :]
        piece[k] = jnp.where(mine, parent[rows, :], sent)

    def subtract(c, _):
        rows = pl.ds(pl.multiple_of(row_level[c] * BLK, BLK), BLK)
        for pick in range(2):
            slot = col_slot[c, pick]
            front[slot, rows, :] = front[slot, rows, :] - got[c, pick * BLK : (pick + 1) * BLK]
            start = 2 * BLK + pick * PIECE
            piece[slot] = piece[slot] - got[c, start : start + PIECE]
        return 0

    lax.fori_loop(0, LEAVES, subtract, 0)
    for i in range(LEAVES):
        spread[i] = piece[0]


def assemble(place, child_map, got, parent, sent):
    return pl.pallas_call(
        assemble_kernel,
        out_shape=(
            jax.ShapeDtypeStruct((8, 4 * BLK, BLK), F32),
            jax.ShapeDtypeStruct((8, PIECE, BLK), F32),
            jax.ShapeDtypeStruct((LEAVES, PIECE, BLK), F32),
        ),
        in_specs=[pl.BlockSpec(memory_space=SMEM)] * 2 + [pl.BlockSpec(memory_space=VMEM)] * 5,
        out_specs=(pl.BlockSpec(memory_space=VMEM),) * 3,
        scratch_shapes=[SMEM((LEAVES,), jnp.int32), SMEM((LEAVES, 2), jnp.int32)],
        compiler_params=pltpu.CompilerParams(vmem_limit_bytes=32 * 2**20),
        cost_estimate=pl.CostEstimate(
            flops=10**6, bytes_accessed=6 * 2**20, transcendentals=0
        ),
    )(place, child_map, got, parent, *sent)


def panel_kernel(place, near, far, l_ref, inv_ref, block, work):
    group = place[1]
    for i, ref in enumerate((near, far)):
        for j in range(2):
            spot = (group & 3) ^ (2 * i + j)
            for x in range(4):
                for y in range(4):
                    rows = slice(y * BLK + x * PIECE, y * BLK + (x + 1) * PIECE)
                    block[spot, rows, :] = ref[j, 4 * x + y]

    def square(r, c):
        rows = slice(r * NB, (r + 1) * NB)
        return jnp.concatenate([block[2 * c, rows, :], block[2 * c + 1, rows, :]], axis=1)

    factor_a, inv_a = diag_block(square(0, 0), work)
    low_left = mul_t(square(1, 0), inv_a)
    factor_b, inv_b = diag_block(square(1, 1) - mul_t(low_left, low_left), work)
    zero = jnp.zeros((NB, NB), F32)
    l_ref[:NB, :NB] = factor_a
    l_ref[:NB, NB:] = zero
    l_ref[NB:, :NB] = low_left
    l_ref[NB:, NB:] = factor_b
    inv_ref[:NB, :NB] = inv_a
    inv_ref[:NB, NB:] = zero
    inv_ref[NB:, :NB] = -mul_n(inv_b, mul_n(low_left, inv_a))
    inv_ref[NB:, NB:] = inv_b


def factor_panel(place, columns):
    return pl.pallas_call(
        panel_kernel,
        out_shape=(jax.ShapeDtypeStruct((PIVOTS, PIVOTS), F32),) * 2,
        in_specs=[pl.BlockSpec(memory_space=SMEM)] + [pl.BlockSpec(memory_space=VMEM)] * 2,
        out_specs=(pl.BlockSpec(memory_space=VMEM),) * 2,
        scratch_shapes=[VMEM((4, PIVOTS, BLK), F32), VMEM((HB, 2 * HB), F32)],
        compiler_params=pltpu.CompilerParams(vmem_limit_bytes=32 * 2**20),
        cost_estimate=pl.CostEstimate(
            flops=25 * 10**9, bytes_accessed=4 * 2**20, transcendentals=0
        ),
    )(place, *columns)


def trailing_kernel(place, front, columns, above, l_ref, inv_ref, out, panel, sem):
    leaf = place[0]
    group = place[1]
    fetch = pltpu.make_async_copy(columns.at[pl.ds(0, 4)], panel, sem)
    fetch.start()
    fetch.wait()
    inverse = inv_ref[...]
    own = jnp.concatenate([panel[i] for i in range(4)], axis=1)
    solved = mul_t(own, inverse)
    solved_parts = left3(solved)
    inverse_parts = left3(inverse)
    row = lax.broadcasted_iota(jnp.int32, (PIVOTS, BLK), 0)
    in_panel = (row < BLK) & (leaf < 4)
    for pair in range(4):
        across = jnp.concatenate(
            [
                jnp.concatenate([above[4 * x + y, 2 * pair], above[4 * x + y, 2 * pair + 1]], axis=1)
                for y in range(4)
                for x in range(4)
            ],
            axis=0,
        )
        across = dot_n(inverse_parts, right3(across, axis=0))
        change = dot_n(solved_parts, right3(across, axis=0))
        for half in range(2):
            k = 2 * pair + half
            value = front[k] - change[:, half * BLK : (half + 1) * BLK]
            out[pl.ds(k, PIVOTS, 8), :] = jnp.where(in_panel, 0.0, value)

    for i in range(4):

        @pl.when(group == i)
        def _():
            out[pl.ds(0, PIVOTS, 8), :] = solved[:, i * BLK : (i + 1) * BLK]

            @pl.when(leaf < 4)
            def _():
                rows = pl.ds(pl.multiple_of((leaf & 3) * BLK, BLK), BLK)
                out[pl.ds(0, BLK, 8), :] = l_ref[rows, i * BLK : (i + 1) * BLK]


def finish(place, front, columns, rows, factor, inverse):
    return pl.pallas_call(
        trailing_kernel,
        out_shape=jax.ShapeDtypeStruct((8 * PIVOTS, BLK), F32),
        in_specs=[
            pl.BlockSpec(memory_space=SMEM),
            pl.BlockSpec(memory_space=VMEM),
            pl.BlockSpec(memory_space=pl.ANY),
        ]
        + [pl.BlockSpec(memory_space=VMEM)] * 3,
        out_specs=pl.BlockSpec(memory_space=VMEM),
        scratch_shapes=[VMEM((4, PIVOTS, BLK), F32), pltpu.SemaphoreType.DMA],
        compiler_params=pltpu.CompilerParams(vmem_limit_bytes=48 * 2**20),
        cost_estimate=pl.CostEstimate(
            flops=5 * 10**9, bytes_accessed=12 * 2**20, transcendentals=0
        ),
    )(place, front, columns, rows, factor, inverse)


def group_swap(x, mask, sources=GROUPS):
    return lax.ppermute(x, GROUP, [(a, a ^ mask) for a in range(sources)])


def panel_columns(x, group):
    near = group_swap(x, 1, 4)
    far = group_swap(x, 4, 4)
    across = group_swap(x, 5, 4)
    mine = group < 4
    both = jnp.stack([jnp.where(mine, x, far), jnp.where(mine, near, across)])
    return both, group_swap(both, 2)


def local(pivot_block, coupling, parent_front, child_map):
    leaf = lax.axis_index("leaf")
    group = lax.axis_index(GROUP)
    place = jnp.stack([leaf, group]).astype(jnp.int32)
    coupled = coupling[0]
    parent = parent_front.reshape(8 * PIVOTS, BLK)
    sent = [
        lax.ppermute(
            parent[to * 8 * PIECE : (to + 1) * 8 * PIECE],
            "leaf",
            [(y, 4 * to + y) for y in range(4)],
        )
        for to in (1, 2, 3)
    ]
    others = [group_swap(coupled, mask) for mask in (1, 5, 4)]
    factor, below, inverses = factor_child(pivot_block[0], coupled)
    below_near, below_across, below_far = solve_rows(factor, inverses, others)
    have = {0: below, 1: below_near, 5: below_across, 4: below_far}
    have.update({mask ^ 2: group_swap(x, 2) for mask, x in list(have.items())})
    products = update_blocks(place, child_map, [have[s] for s in range(GROUPS)])
    got = lax.all_to_all(products, "leaf", split_axis=0, concat_axis=0, tiled=True)
    front, piece, spread = assemble(place, child_map, got, parent, sent)
    diag_rows = lax.all_to_all(spread, "leaf", split_axis=0, concat_axis=0, tiled=True)
    rows = lax.all_gather(piece, "leaf", axis=0)
    columns = lax.all_gather(front[0], GROUP, axis=0)
    panel_factor, panel_inverse = factor_panel(place, panel_columns(diag_rows, group))
    result = finish(place, front, columns, rows, panel_factor, panel_inverse)
    factor_own = lax.dynamic_slice_in_dim(factor, group * NB, NB, 0)
    return (
        factor_own[None],
        below[None],
        result.reshape(4, 1, BLK, 8, 1, BLK),
    )


def solution(mesh):
    return jax.shard_map(
        local,
        mesh=mesh,
        in_specs=(
            P("leaf", None, None),
            P("leaf", GROUP, None),
            P(None, "leaf", None, None, GROUP, None),
            P(),
        ),
        out_specs=(
            P("leaf", GROUP, None),
            P("leaf", GROUP, None),
            P(None, "leaf", None, None, GROUP, None),
        ),
        check_vma=False,
    )
```

```python
import functools

import jax
import jax.numpy as jnp
from jax import lax
from jax.experimental import pallas as pl
from jax.experimental.pallas import tpu as pltpu
from jax.sharding import PartitionSpec as P

F32 = jnp.float32
BF16 = jnp.bfloat16
S = 2048
BLK = 128
PIVOTS = 512
LEAVES = 16
GROUPS = 8
NB = 256
HB = 128
CORNER = 16
PIECE = 32
SUB = 32
STEPS = S // NB
VMEM = pltpu.VMEM
SMEM = pltpu.SMEM
GROUP = ("row", "col")


def dot_t(a, b):
    return lax.dot_general(a, b, (((1,), (1,)), ((), ())), preferred_element_type=F32)


def dot_n(a, b):
    return lax.dot_general(a, b, (((1,), (0,)), ((), ())), preferred_element_type=F32)


def halves(x):
    high = x.astype(BF16)
    low = (x - high.astype(F32)).astype(BF16)
    return high, low


def left3(x, axis=1):
    high, low = halves(x)
    return jnp.concatenate([high, high, low], axis=axis)


def right3(x, axis=1):
    high, low = halves(x)
    return jnp.concatenate([high, low, high], axis=axis)


def mul_t(a, b):
    return dot_t(left3(a), right3(b))


def mul_n(a, b):
    return dot_n(left3(a), right3(b, axis=0))


def eliminate(rows, base):
    groups = SUB // 8
    sub = lax.broadcasted_iota(jnp.int32, (8, HB), 0)
    state = [
        [rows[8 * a : 8 * a + 8, HB * h : HB * h + HB] for h in range(2)] for a in range(groups)
    ]
    cols = [
        [
            jnp.broadcast_to(rows[8 * a : 8 * a + 8, base + j : base + j + 1], (8, HB))
            if a >= j // 8
            else None
            for a in range(groups)
        ]
        for j in range(SUB)
    ]
    for k in range(SUB):
        own, line = divmod(k, 8)
        inv = lax.rsqrt(jnp.broadcast_to(cols[k][own][line : line + 1, :], (8, HB)))
        scaled = [cols[k][a] * inv if a >= own else None for a in range(groups)]
        below = list(scaled)
        below[own] = jnp.where(sub > line, scaled[own], 0.0)
        for j in range(k + 1, SUB):
            at, spot = divmod(j, 8)
            across = jnp.broadcast_to(scaled[at][spot : spot + 1, :], (8, HB))
            for a in range(at, groups):
                cols[j][a] = cols[j][a] - below[a] * across
        for h in range(2):
            pivot_row = jnp.broadcast_to(state[own][h][line : line + 1, :], (8, HB)) * inv
            state[own][h] = jnp.where(
                sub == line, pivot_row, state[own][h] - below[own] * pivot_row
            )
            for a in range(own + 1, groups):
                state[a][h] = state[a][h] - below[a] * pivot_row
    return jnp.concatenate([jnp.concatenate(pair, axis=1) for pair in state], axis=0)


def diag_small(block, work):
    row = lax.broadcasted_iota(jnp.int32, (HB, HB), 0)
    col = lax.broadcasted_iota(jnp.int32, (HB, HB), 1)
    work[:, :HB] = block
    work[:, HB:] = jnp.where(row == col, 1.0, 0.0)
    for base in range(0, HB, SUB):
        rows = eliminate(work[base : base + SUB, :], base)
        work[base : base + SUB, :] = rows
        after = base + SUB
        if after < HB:
            high = rows.astype(BF16).astype(F32)
            low = rows - high
            left = jnp.concatenate([high[:, :HB], high[:, :HB], low[:, :HB]], axis=0).astype(BF16)
            right = jnp.concatenate([high, low, high], axis=0).astype(BF16)
            product = lax.dot_general(
                left, right, (((0,), (0,)), ((), ())), preferred_element_type=F32
            )
            work[after:, :] = work[after:, :] - product[after:, :]
    return jnp.where(col >= row, work[:, :HB], 0.0), work[:, HB:]


def diag_block(block, work):
    upper_a, inv_a = diag_small(block[:HB, :HB], work)
    low_left = mul_t(block[HB:, :HB], inv_a)
    upper_b, inv_b = diag_small(block[HB:, HB:] - mul_t(low_left, low_left), work)
    inv_low = -mul_n(inv_b, mul_n(low_left, inv_a))
    zero = jnp.zeros((HB, HB), F32)
    factor = jnp.concatenate(
        [
            jnp.concatenate([upper_a.T, zero], axis=1),
            jnp.concatenate([low_left, upper_b.T], axis=1),
        ],
        axis=0,
    )
    inverse = jnp.concatenate(
        [
            jnp.concatenate([inv_a, zero], axis=1),
            jnp.concatenate([inv_low, inv_b], axis=1),
        ],
        axis=0,
    )
    return factor, inverse


def part(i):
    return pl.ds(pl.multiple_of(i * NB, NB), NB)


def factor_kernel(p_ref, c_ref, l_ref, b_ref, inv_ref, work, left, right):
    def load_row(i, _):
        def load(k, _):
            l_ref[part(i), part(k)] = p_ref[part(i), part(k)].astype(F32)
            return 0

        def clear(k, _):
            l_ref[part(i), part(k)] = jnp.zeros((NB, NB), F32)
            return 0

        lax.fori_loop(0, i + 1, load, 0)
        lax.fori_loop(i + 1, STEPS, clear, 0)
        return 0

    lax.fori_loop(0, STEPS, load_row, 0)
    b_ref[...] = c_ref[...]

    def step(j, _):
        factor, inverse = diag_block(l_ref[part(j), part(j)], work)
        l_ref[part(j), part(j)] = factor
        inv_ref[j] = inverse
        inverse_parts = right3(inverse)
        own = dot_t(left3(b_ref[:, part(j)]), inverse_parts)
        b_ref[:, part(j)] = own
        own_parts = left3(own)

        def panel(i, _):
            x = dot_t(left3(l_ref[part(i), part(j)]), inverse_parts)
            l_ref[part(i), part(j)] = x
            left[part(i), :] = left3(x)
            right[part(i), :] = right3(x)
            return 0

        lax.fori_loop(j + 1, STEPS, panel, 0)

        def trail(k, _):
            b_ref[:, part(k)] = b_ref[:, part(k)] - dot_t(own_parts, right[part(k), :])

            def trail_row(i, _):
                l_ref[part(i), part(k)] = l_ref[part(i), part(k)] - dot_t(
                    left[part(i), :], right[part(k), :]
                )
                return 0

            lax.fori_loop(k, STEPS, trail_row, 0)
            return 0

        lax.fori_loop(j + 1, STEPS, trail, 0)
        return 0

    lax.fori_loop(0, STEPS, step, 0)


def factor_child(pivot, coupling):
    return pl.pallas_call(
        factor_kernel,
        out_shape=(
            jax.ShapeDtypeStruct((S, S), F32),
            jax.ShapeDtypeStruct((NB, S), F32),
            jax.ShapeDtypeStruct((STEPS, NB, NB), F32),
        ),
        in_specs=[pl.BlockSpec(memory_space=VMEM)] * 2,
        out_specs=(pl.BlockSpec(memory_space=VMEM),) * 3,
        scratch_shapes=[
            VMEM((HB, 2 * HB), F32),
            VMEM((S, 3 * NB), BF16),
            VMEM((S, 3 * NB), BF16),
        ],
        compiler_params=pltpu.CompilerParams(vmem_limit_bytes=56 * 2**20),
        cost_estimate=pl.CostEstimate(
            flops=150 * 10**9, bytes_accessed=30 * 2**20, transcendentals=0
        ),
    )(pivot, coupling)


def solve_kernel(count, after, l_hbm, inv_ref, *refs):
    ins = refs[:count]
    outs = refs[count + after : 2 * count + after]
    l_vmem, c_vmem, high, low, sems = refs[2 * count + after :]

    def l_copy(j):
        where = (pl.ds(j * NB, NB), pl.ds(0, (j + 1) * NB))
        return pltpu.make_async_copy(l_hbm.at[where], l_vmem.at[where], sems.at[j])

    def c_copy(j, i):
        cols = pl.ds(j * NB, NB)
        return pltpu.make_async_copy(
            ins[i].at[:, cols], c_vmem.at[pl.ds(i * NB, NB), cols], sems.at[STEPS + j * count + i]
        )

    for j in range(STEPS):
        l_copy(j).start()
        for i in range(count):
            c_copy(j, i).start()
    for j in range(STEPS):
        l_copy(j).wait()
        for i in range(count):
            c_copy(j, i).wait()
        rhs = c_vmem[:, j * NB : (j + 1) * NB]
        if j:
            before = slice(0, j * NB)
            f_high, f_low = halves(l_vmem[j * NB : (j + 1) * NB, before])
            rhs = rhs - (
                dot_t(high[:, before], f_high)
                + dot_t(high[:, before], f_low)
                + dot_t(low[:, before], f_high)
            )
        x = mul_t(rhs, inv_ref[j])
        x_high, x_low = halves(x)
        high[:, j * NB : (j + 1) * NB] = x_high
        low[:, j * NB : (j + 1) * NB] = x_low
        for i in range(count):
            outs[i][:, j * NB : (j + 1) * NB] = x[i * NB : (i + 1) * NB]


def solve_rows(factor, inverses, rows, after=()):
    count = len(rows)
    return pl.pallas_call(
        functools.partial(solve_kernel, count, len(after)),
        out_shape=(jax.ShapeDtypeStruct((NB, S), F32),) * count,
        in_specs=[pl.BlockSpec(memory_space=pl.ANY), pl.BlockSpec(memory_space=VMEM)]
        + [pl.BlockSpec(memory_space=pl.ANY)] * (count + len(after)),
        out_specs=(pl.BlockSpec(memory_space=VMEM),) * count,
        scratch_shapes=[
            VMEM((S, S), F32),
            VMEM((count * NB, S), F32),
            VMEM((count * NB, S), BF16),
            VMEM((count * NB, S), BF16),
            pltpu.SemaphoreType.DMA((STEPS * (1 + count),)),
        ],
        compiler_params=pltpu.CompilerParams(vmem_limit_bytes=56 * 2**20),
        cost_estimate=pl.CostEstimate(
            flops=count * 7 * 10**9, bytes_accessed=24 * 2**20, transcendentals=0
        ),
    )(factor, inverses, *rows, *after)


def update_kernel(place, map_ref, *refs):
    ins = refs[:GROUPS]
    out, corner, tiles, chosen, high, low, sems = refs[GROUPS + 1 :]
    leaf = place[0]
    group = place[1]

    def keep(y):
        level = jnp.int32(0)
        for t in range(LEAVES):
            block = map_ref[leaf, t]
            level = jnp.where((block & (LEAVES - 1)) == y, block >> 4, level)
        return jnp.where(level == 0, 1.0, 0.0).astype(F32)

    for s in range(GROUPS):
        for half in range(2):
            tile = (group ^ s) * 2 + half
            dest = lax.rem(map_ref[leaf, tile], LEAVES)
            rows = pl.ds(half * BLK, BLK)
            pltpu.make_async_copy(ins[s].at[rows, :], tiles.at[dest], sems.at[dest]).start()
            for pick in range(2):

                @pl.when(dest == group + pick * GROUPS)
                def _():
                    pltpu.make_async_copy(
                        ins[s].at[rows, :],
                        chosen.at[pl.ds(pick * BLK, BLK), :],
                        sems.at[LEAVES + pick],
                    ).start()

    for pick in range(2):
        pltpu.make_async_copy(
            ins[0].at[pl.ds(0, BLK), :],
            chosen.at[pl.ds(pick * BLK, BLK), :],
            sems.at[LEAVES + pick],
        ).wait()
    high[...], low[...] = halves(chosen[...])
    together = 4

    def tile_group(q, _):
        for t in range(together):
            pltpu.make_async_copy(
                ins[0].at[pl.ds(0, BLK), :],
                tiles.at[q * together + t],
                sems.at[q * together + t],
            ).wait()
        rows = tiles[pl.ds(q * together, together)].reshape(together * BLK, S)
        r_high, r_low = halves(rows)
        product = (
            dot_t(r_high, high[...]) + dot_t(r_high, low[...]) + dot_t(r_low, high[...])
        )
        for t in range(together):
            for pick in range(2):
                out[q * together + t, pick * BLK : (pick + 1) * BLK] = product[
                    t * BLK : (t + 1) * BLK, pick * BLK : (pick + 1) * BLK
                ]

        @pl.when(q == 0)
        def _():
            for y in range(together):
                kept = keep(y)
                for x in range(4):
                    for pick in range(2):
                        start = 2 * BLK + pick * PIECE
                        out[4 * x + y, start : start + PIECE] = kept * product[
                            y * BLK + x * PIECE : y * BLK + (x + 1) * PIECE,
                            pick * BLK : (pick + 1) * BLK,
                        ]
            down = 2 * (group >> 2)
            right = group & 3
            square = keep(right) * mul_t(
                tiles[pl.ds(down, 2)].reshape(2 * BLK, S), tiles[right]
            )
            for i in range(LEAVES):
                corner[i] = keep(down + i // 8) * square[i * CORNER : (i + 1) * CORNER]

        return 0

    lax.fori_loop(0, LEAVES // together, tile_group, 0)


def update_blocks(place, child_map, rows, after):
    return pl.pallas_call(
        update_kernel,
        out_shape=(
            jax.ShapeDtypeStruct((LEAVES, 2 * (BLK + PIECE), BLK), F32),
            jax.ShapeDtypeStruct((LEAVES, CORNER, BLK), F32),
        ),
        in_specs=[pl.BlockSpec(memory_space=SMEM)] * 2
        + [pl.BlockSpec(memory_space=pl.ANY)] * (GROUPS + 1),
        out_specs=(pl.BlockSpec(memory_space=VMEM),) * 2,
        scratch_shapes=[
            VMEM((LEAVES, BLK, S), F32),
            VMEM((2 * BLK, S), F32),
            VMEM((2 * BLK, S), BF16),
            VMEM((2 * BLK, S), BF16),
            pltpu.SemaphoreType.DMA((LEAVES + 2,)),
        ],
        compiler_params=pltpu.CompilerParams(vmem_limit_bytes=56 * 2**20),
        cost_estimate=pl.CostEstimate(
            flops=8 * 10**9, bytes_accessed=20 * 2**20, transcendentals=0
        ),
    )(place, child_map, *rows, after)


def assemble_kernel(
    place, map_ref, got, parent, p1, p2, p3, _, front, column, spread, piece, row_level, col_slot
):
    leaf = place[0]
    group = place[1]

    def find(c, _):
        level = jnp.int32(0)
        slots = [jnp.int32(0), jnp.int32(0)]
        for t in range(LEAVES):
            block = map_ref[c, t]
            residue = block & (LEAVES - 1)
            level = jnp.where(residue == leaf, block >> 4, level)
            for pick in range(2):
                slots[pick] = jnp.where(
                    residue == group + pick * GROUPS, block >> 3, slots[pick]
                )
        row_level[c] = level
        for pick in range(2):
            col_slot[c, pick] = slots[pick]
        return 0

    lax.fori_loop(0, LEAVES, find, 0)
    mine = leaf < 4
    for k in range(8):
        front[k] = parent[pl.ds(k, 4 * BLK, 8), :]
        rows = pl.ds(k, PIECE, 8)
        sent = p1[rows, :] + p2[rows, :] + p3[rows, :]
        piece[k] = jnp.where(mine, parent[rows, :], sent)

    def subtract(c, _):
        rows = pl.ds(pl.multiple_of(row_level[c] * BLK, BLK), BLK)
        for pick in range(2):
            slot = col_slot[c, pick]
            front[slot, rows, :] = front[slot, rows, :] - got[c, pick * BLK : (pick + 1) * BLK]
            start = 2 * BLK + pick * PIECE
            piece[slot] = piece[slot] - got[c, start : start + PIECE]
        return 0

    lax.fori_loop(0, LEAVES, subtract, 0)
    for i in range(LEAVES):
        spread[i] = piece[...]
    column[...] = front[0]


def assemble(place, child_map, got, parent, sent, after):
    return pl.pallas_call(
        assemble_kernel,
        out_shape=(
            jax.ShapeDtypeStruct((8, 4 * BLK, BLK), F32),
            jax.ShapeDtypeStruct((4 * BLK, BLK), F32),
            jax.ShapeDtypeStruct((LEAVES, 8, PIECE, BLK), F32),
        ),
        in_specs=[pl.BlockSpec(memory_space=SMEM)] * 2
        + [pl.BlockSpec(memory_space=VMEM)] * 5
        + [pl.BlockSpec(memory_space=pl.ANY)],
        out_specs=(pl.BlockSpec(memory_space=VMEM),) * 3,
        scratch_shapes=[
            VMEM((8, PIECE, BLK), F32),
            SMEM((LEAVES,), jnp.int32),
            SMEM((LEAVES, 2), jnp.int32),
        ],
        compiler_params=pltpu.CompilerParams(vmem_limit_bytes=32 * 2**20),
        cost_estimate=pl.CostEstimate(
            flops=10**6, bytes_accessed=6 * 2**20, transcendentals=0
        ),
    )(place, child_map, got, parent, *sent, after)


def panel_kernel(initial, sums, l_ref, inv_ref, block, work, sem):
    fetch = pltpu.make_async_copy(initial.at[pl.ds(0, 4)], block, sem)
    fetch.start()
    fetch.wait()
    for r in range(LEAVES):
        for g in range(GROUPS):
            start = (g // 4) * NB + r * CORNER
            rows = slice(start, start + CORNER)
            block[g % 4, rows, :] = block[g % 4, rows, :] - sums[r * GROUPS + g]

    def square(r, c):
        rows = slice(r * NB, (r + 1) * NB)
        return jnp.concatenate([block[2 * c, rows, :], block[2 * c + 1, rows, :]], axis=1)

    factor_a, inv_a = diag_block(square(0, 0), work)
    low_left = mul_t(square(1, 0), inv_a)
    factor_b, inv_b = diag_block(square(1, 1) - mul_t(low_left, low_left), work)
    zero = jnp.zeros((NB, NB), F32)
    l_ref[:NB, :NB] = factor_a
    l_ref[:NB, NB:] = zero
    l_ref[NB:, :NB] = low_left
    l_ref[NB:, NB:] = factor_b
    inv_ref[:NB, :NB] = inv_a
    inv_ref[:NB, NB:] = zero
    inv_ref[NB:, :NB] = -mul_n(inv_b, mul_n(low_left, inv_a))
    inv_ref[NB:, NB:] = inv_b


def factor_panel(initial, sums):
    return pl.pallas_call(
        panel_kernel,
        out_shape=(jax.ShapeDtypeStruct((PIVOTS, PIVOTS), F32),) * 2,
        in_specs=[pl.BlockSpec(memory_space=pl.ANY), pl.BlockSpec(memory_space=VMEM)],
        out_specs=(pl.BlockSpec(memory_space=VMEM),) * 2,
        scratch_shapes=[
            VMEM((4, PIVOTS, BLK), F32),
            VMEM((HB, 2 * HB), F32),
            pltpu.SemaphoreType.DMA,
        ],
        compiler_params=pltpu.CompilerParams(vmem_limit_bytes=32 * 2**20),
        cost_estimate=pl.CostEstimate(
            flops=25 * 10**9, bytes_accessed=4 * 2**20, transcendentals=0
        ),
    )(initial, sums)


def trailing_kernel(place, front, here, there, above, l_ref, inv_ref, out, panel):
    leaf = place[0]
    group = place[1]
    for i, ref in enumerate((here, there)):
        for j in range(2):
            panel[(group & 3) ^ (2 * i + j)] = ref[j]
    inverse = inv_ref[...]
    own = jnp.concatenate([panel[i] for i in range(4)], axis=1)
    solved = mul_t(own, inverse)
    solved_parts = left3(solved)
    inverse_parts = left3(inverse)
    row = lax.broadcasted_iota(jnp.int32, (PIVOTS, BLK), 0)
    in_panel = (row < BLK) & (leaf < 4)
    for pair in range(4):
        across = jnp.concatenate(
            [
                jnp.concatenate([above[4 * x + y, 2 * pair], above[4 * x + y, 2 * pair + 1]], axis=1)
                for y in range(4)
                for x in range(4)
            ],
            axis=0,
        )
        across = dot_n(inverse_parts, right3(across, axis=0))
        change = dot_n(solved_parts, right3(across, axis=0))
        for half in range(2):
            k = 2 * pair + half
            value = front[k] - change[:, half * BLK : (half + 1) * BLK]
            out[pl.ds(k, PIVOTS, 8), :] = jnp.where(in_panel, 0.0, value)

    for i in range(4):

        @pl.when(group == i)
        def _():
            out[pl.ds(0, PIVOTS, 8), :] = solved[:, i * BLK : (i + 1) * BLK]

            @pl.when(leaf < 4)
            def _():
                rows = pl.ds(pl.multiple_of((leaf & 3) * BLK, BLK), BLK)
                out[pl.ds(0, BLK, 8), :] = l_ref[rows, i * BLK : (i + 1) * BLK]


def finish(place, front, columns, rows, factor, inverse):
    return pl.pallas_call(
        trailing_kernel,
        out_shape=jax.ShapeDtypeStruct((8 * PIVOTS, BLK), F32),
        in_specs=[pl.BlockSpec(memory_space=SMEM)] + [pl.BlockSpec(memory_space=VMEM)] * 6,
        out_specs=pl.BlockSpec(memory_space=VMEM),
        scratch_shapes=[VMEM((4, PIVOTS, BLK), F32)],
        compiler_params=pltpu.CompilerParams(vmem_limit_bytes=48 * 2**20),
        cost_estimate=pl.CostEstimate(
            flops=5 * 10**9, bytes_accessed=12 * 2**20, transcendentals=0
        ),
    )(place, front, *columns, rows, factor, inverse)


def group_swap(x, mask, sources=GROUPS):
    return lax.ppermute(x, GROUP, [(a, a ^ mask) for a in range(sources)])


def panel_columns(x, group):
    near = group_swap(x, 1, 4)
    far = group_swap(x, 4, 4)
    across = group_swap(x, 5, 4)
    mine = group < 4
    both = jnp.stack([jnp.where(mine, x, far), jnp.where(mine, near, across)])
    return both, group_swap(both, 2)


def local(pivot_block, coupling, parent_front, child_map):
    leaf = lax.axis_index("leaf")
    group = lax.axis_index(GROUP)
    place = jnp.stack([leaf, group]).astype(jnp.int32)
    coupled = coupling[0]
    parent = parent_front.reshape(8 * PIVOTS, BLK)
    sent = [
        lax.ppermute(
            parent[to * 8 * PIECE : (to + 1) * 8 * PIECE],
            "leaf",
            [(y, 4 * to + y) for y in range(4)],
        )
        for to in (1, 2, 3)
    ]
    corner = parent.reshape(PIVOTS, 8, BLK)[:BLK, 0]
    corner_rows = lax.all_gather(corner, "leaf", axis=0)[:4].reshape(PIVOTS, BLK)
    near, across, far = [group_swap(coupled, mask) for mask in (1, 5, 4)]
    factor, below, inverses = factor_child(pivot_block[0], coupled)
    near, across = solve_rows(factor, inverses, [near, across], (*sent, corner_rows))
    corner_all = lax.all_gather(corner_rows, GROUP, axis=0)
    (far,) = solve_rows(factor, inverses, [far])
    have = {0: below, 1: near, 5: across, 4: far}
    have.update({mask ^ 2: group_swap(x, 2) for mask, x in list(have.items())})
    products, corner_part = update_blocks(
        place, child_map, [have[s] for s in range(GROUPS)], corner_all
    )
    got = lax.all_to_all(products, "leaf", split_axis=0, concat_axis=0, tiled=True)
    corner_got = lax.all_to_all(corner_part, "leaf", split_axis=0, concat_axis=0, tiled=True)
    corner_sum = jnp.broadcast_to(
        jnp.sum(corner_got, axis=0)[None], (LEAVES * GROUPS, CORNER, BLK)
    )
    corner_sums = lax.all_to_all(
        corner_sum, ("leaf", "row", "col"), split_axis=0, concat_axis=0, tiled=True
    )
    front, column, spread = assemble(place, child_map, got, parent, sent, corner_sums)
    rows = lax.all_to_all(spread, "leaf", split_axis=0, concat_axis=0, tiled=True)
    columns = panel_columns(column, group)
    panel_factor, panel_inverse = factor_panel(corner_all, corner_sums)
    result = finish(place, front, columns, rows, panel_factor, panel_inverse)
    factor_own = lax.dynamic_slice_in_dim(factor, group * NB, NB, 0)
    return (
        factor_own[None],
        below[None],
        result.reshape(4, 1, BLK, 8, 1, BLK),
    )


def solution(mesh):
    return jax.shard_map(
        local,
        mesh=mesh,
        in_specs=(
            P("leaf", None, None),
            P("leaf", GROUP, None),
            P(None, "leaf", None, None, GROUP, None),
            P(),
        ),
        out_specs=(
            P("leaf", GROUP, None),
            P("leaf", GROUP, None),
            P(None, "leaf", None, None, GROUP, None),
        ),
        check_vma=False,
    )
```

```python
import functools

import jax
import jax.numpy as jnp
from jax import lax
from jax.experimental import pallas as pl
from jax.experimental.pallas import tpu as pltpu
from jax.sharding import PartitionSpec as P

F32 = jnp.float32
BF16 = jnp.bfloat16
S = 2048
BLK = 128
PIVOTS = 512
LEAVES = 16
GROUPS = 8
NB = 256
HB = 128
SUB = 32
STEPS = S // NB
VMEM = pltpu.VMEM
SMEM = pltpu.SMEM
GROUP = ("row", "col")


def dot_t(a, b):
    return lax.dot_general(a, b, (((1,), (1,)), ((), ())), preferred_element_type=F32)


def dot_n(a, b):
    return lax.dot_general(a, b, (((1,), (0,)), ((), ())), preferred_element_type=F32)


def halves(x):
    high = x.astype(BF16)
    low = (x - high.astype(F32)).astype(BF16)
    return high, low


def left3(x, axis=1):
    high, low = halves(x)
    return jnp.concatenate([high, high, low], axis=axis)


def right3(x, axis=1):
    high, low = halves(x)
    return jnp.concatenate([high, low, high], axis=axis)


def mul_t(a, b):
    return dot_t(left3(a), right3(b))


def mul_n(a, b):
    return dot_n(left3(a), right3(b, axis=0))


def eliminate(rows, base):
    groups = SUB // 8
    sub = lax.broadcasted_iota(jnp.int32, (8, HB), 0)
    state = [
        [rows[8 * a : 8 * a + 8, HB * h : HB * h + HB] for h in range(2)] for a in range(groups)
    ]
    cols = [
        [
            jnp.broadcast_to(rows[8 * a : 8 * a + 8, base + j : base + j + 1], (8, HB))
            if a >= j // 8
            else None
            for a in range(groups)
        ]
        for j in range(SUB)
    ]
    for k in range(SUB):
        own, line = divmod(k, 8)
        inv = lax.rsqrt(jnp.broadcast_to(cols[k][own][line : line + 1, :], (8, HB)))
        scaled = [cols[k][a] * inv if a >= own else None for a in range(groups)]
        below = list(scaled)
        below[own] = jnp.where(sub > line, scaled[own], 0.0)
        for j in range(k + 1, SUB):
            at, spot = divmod(j, 8)
            across = jnp.broadcast_to(scaled[at][spot : spot + 1, :], (8, HB))
            for a in range(at, groups):
                cols[j][a] = cols[j][a] - below[a] * across
        for h in range(2):
            pivot_row = jnp.broadcast_to(state[own][h][line : line + 1, :], (8, HB)) * inv
            state[own][h] = jnp.where(
                sub == line, pivot_row, state[own][h] - below[own] * pivot_row
            )
            for a in range(own + 1, groups):
                state[a][h] = state[a][h] - below[a] * pivot_row
    return jnp.concatenate([jnp.concatenate(pair, axis=1) for pair in state], axis=0)


def diag_small(block, work):
    row = lax.broadcasted_iota(jnp.int32, (HB, HB), 0)
    col = lax.broadcasted_iota(jnp.int32, (HB, HB), 1)
    work[:, :HB] = block
    work[:, HB:] = jnp.where(row == col, 1.0, 0.0)
    for base in range(0, HB, SUB):
        rows = eliminate(work[base : base + SUB, :], base)
        work[base : base + SUB, :] = rows
        after = base + SUB
        if after < HB:
            high = rows.astype(BF16).astype(F32)
            low = rows - high
            left = jnp.concatenate([high[:, :HB], high[:, :HB], low[:, :HB]], axis=0).astype(BF16)
            right = jnp.concatenate([high, low, high], axis=0).astype(BF16)
            product = lax.dot_general(
                left, right, (((0,), (0,)), ((), ())), preferred_element_type=F32
            )
            work[after:, :] = work[after:, :] - product[after:, :]
    return jnp.where(col >= row, work[:, :HB], 0.0), work[:, HB:]


def diag_block(block, work):
    upper_a, inv_a = diag_small(block[:HB, :HB], work)
    low_left = mul_t(block[HB:, :HB], inv_a)
    upper_b, inv_b = diag_small(block[HB:, HB:] - mul_t(low_left, low_left), work)
    inv_low = -mul_n(inv_b, mul_n(low_left, inv_a))
    zero = jnp.zeros((HB, HB), F32)
    factor = jnp.concatenate(
        [
            jnp.concatenate([upper_a.T, zero], axis=1),
            jnp.concatenate([low_left, upper_b.T], axis=1),
        ],
        axis=0,
    )
    inverse = jnp.concatenate(
        [
            jnp.concatenate([inv_a, zero], axis=1),
            jnp.concatenate([inv_low, inv_b], axis=1),
        ],
        axis=0,
    )
    return factor, inverse


def part(i):
    return pl.ds(pl.multiple_of(i * NB, NB), NB)


OWN = STEPS
TALL = 4
TALL_PANEL = 4
ROWS = (OWN + max(TALL, TALL_PANEL)) * NB


def tall(i, count):
    return pl.ds(pl.multiple_of(i * NB, NB), count * NB)


def factor_kernel(
    place, p_hbm, c_hbm, l_hbm, own_hbm, b_hbm, inv_ref, p_vmem, full, work, left, right, sems
):
    def p_copy(i):
        where = (pl.ds(i * NB, NB), pl.ds(0, (i + 1) * NB))
        return pltpu.make_async_copy(p_hbm.at[where], p_vmem.at[where], sems.at[i])

    def l_copy(j):
        where = (pl.ds(j * NB, S - j * NB), pl.ds(j * NB, NB))
        return pltpu.make_async_copy(full.at[where], l_hbm.at[where], sems.at[STEPS + 1 + j])

    c_copy = pltpu.make_async_copy(c_hbm, full.at[pl.ds(S, NB), :], sems.at[STEPS])
    for i in range(STEPS):
        p_copy(i).start()
    c_copy.start()
    for i in range(STEPS):
        p_copy(i).wait()
        rows = slice(i * NB, (i + 1) * NB)
        for k in range(i + 1):
            cols = slice(k * NB, (k + 1) * NB)
            full[rows, cols] = p_vmem[rows, cols].astype(F32)
        if i + 1 < STEPS:
            full[rows, (i + 1) * NB :] = jnp.zeros((NB, S - (i + 1) * NB), F32)
    c_copy.wait()

    def step(j, _):
        factor, inverse = diag_block(full[part(j), part(j)], work)
        full[part(j), part(j)] = factor
        inv_ref[j] = inverse
        inverse_parts = right3(inverse)

        def panel(t, _):
            rows = tall(j + 1 + t * TALL_PANEL, TALL_PANEL)
            x = dot_t(left3(full[rows, part(j)]), inverse_parts)
            full[rows, part(j)] = x
            left[rows, :] = left3(x)
            right[rows, :] = right3(x)
            return 0

        lax.fori_loop(0, (OWN - j + TALL_PANEL - 1) // TALL_PANEL, panel, 0)
        for i in range(STEPS):

            @pl.when(j == i)
            def _():
                l_copy(i).start()

        def trail(k, _):
            def trail_rows(t, _):
                rows = tall(k + t * TALL, TALL)
                full[rows, part(k)] = full[rows, part(k)] - dot_t(left[rows, :], right[part(k), :])
                return 0

            lax.fori_loop(0, (OWN + 1 - k + TALL - 1) // TALL, trail_rows, 0)
            return 0

        lax.fori_loop(j + 1, STEPS, trail, 0)
        return 0

    lax.fori_loop(0, STEPS, step, 0)
    b_copy = pltpu.make_async_copy(full.at[pl.ds(S, NB), :], b_hbm, sems.at[STEPS])
    own_copy = pltpu.make_async_copy(full.at[part(place[1]), :], own_hbm, sems.at[0])
    b_copy.start()
    own_copy.start()
    for j in range(STEPS):
        l_copy(j).wait()
    b_copy.wait()
    own_copy.wait()


def factor_child(place, pivot, coupling):
    return pl.pallas_call(
        factor_kernel,
        out_shape=(
            jax.ShapeDtypeStruct((S, S), F32),
            jax.ShapeDtypeStruct((NB, S), F32),
            jax.ShapeDtypeStruct((NB, S), F32),
            jax.ShapeDtypeStruct((STEPS, NB, NB), F32),
        ),
        in_specs=[pl.BlockSpec(memory_space=SMEM)] + [pl.BlockSpec(memory_space=pl.ANY)] * 2,
        out_specs=(pl.BlockSpec(memory_space=pl.ANY),) * 3 + (pl.BlockSpec(memory_space=VMEM),),
        scratch_shapes=[
            VMEM((S, S), BF16),
            VMEM((ROWS, S), F32),
            VMEM((HB, 2 * HB), F32),
            VMEM((ROWS, 3 * NB), BF16),
            VMEM((ROWS, 3 * NB), BF16),
            pltpu.SemaphoreType.DMA((2 * STEPS + 1,)),
        ],
        compiler_params=pltpu.CompilerParams(vmem_limit_bytes=58 * 2**20),
        cost_estimate=pl.CostEstimate(
            flops=100 * 10**9, bytes_accessed=30 * 2**20, transcendentals=0
        ),
    )(place, pivot, coupling)


def solve_kernel(count, after, l_hbm, inv_ref, *refs):
    ins = refs[:count]
    outs = refs[count + after : 2 * count + after]
    l_vmem, c_vmem, high, low, sems = refs[2 * count + after :]

    def l_copy(j):
        where = (pl.ds(j * NB, NB), pl.ds(0, (j + 1) * NB))
        return pltpu.make_async_copy(l_hbm.at[where], l_vmem.at[where], sems.at[j])

    def c_copy(j, i):
        cols = pl.ds(j * NB, NB)
        return pltpu.make_async_copy(
            ins[i].at[:, cols], c_vmem.at[pl.ds(i * NB, NB), cols], sems.at[STEPS + j * count + i]
        )

    for j in range(STEPS):
        l_copy(j).start()
        for i in range(count):
            c_copy(j, i).start()
    for j in range(STEPS):
        l_copy(j).wait()
        for i in range(count):
            c_copy(j, i).wait()
        rhs = c_vmem[:, j * NB : (j + 1) * NB]
        if j:
            before = slice(0, j * NB)
            f_high, f_low = halves(l_vmem[j * NB : (j + 1) * NB, before])
            rhs = rhs - (
                dot_t(high[:, before], f_high)
                + dot_t(high[:, before], f_low)
                + dot_t(low[:, before], f_high)
            )
        x = mul_t(rhs, inv_ref[j])
        x_high, x_low = halves(x)
        high[:, j * NB : (j + 1) * NB] = x_high
        low[:, j * NB : (j + 1) * NB] = x_low
        for i in range(count):
            outs[i][:, j * NB : (j + 1) * NB] = x[i * NB : (i + 1) * NB]


def solve_rows(factor, inverses, rows, after=()):
    count = len(rows)
    return pl.pallas_call(
        functools.partial(solve_kernel, count, len(after)),
        out_shape=(jax.ShapeDtypeStruct((NB, S), F32),) * count,
        in_specs=[pl.BlockSpec(memory_space=pl.ANY), pl.BlockSpec(memory_space=VMEM)]
        + [pl.BlockSpec(memory_space=pl.ANY)] * (count + len(after)),
        out_specs=(pl.BlockSpec(memory_space=VMEM),) * count,
        scratch_shapes=[
            VMEM((S, S), F32),
            VMEM((count * NB, S), F32),
            VMEM((count * NB, S), BF16),
            VMEM((count * NB, S), BF16),
            pltpu.SemaphoreType.DMA((STEPS * (1 + count),)),
        ],
        compiler_params=pltpu.CompilerParams(vmem_limit_bytes=56 * 2**20),
        cost_estimate=pl.CostEstimate(
            flops=count * 7 * 10**9, bytes_accessed=24 * 2**20, transcendentals=0
        ),
    )(factor, inverses, *rows, *after)


def update_kernel(place, map_ref, *refs):
    ins = refs[:GROUPS]
    out, tiles, chosen, high, low, sems = refs[GROUPS:]
    leaf = place[0]
    group = place[1]
    for s in range(GROUPS):
        for half in range(2):
            tile = (group ^ s) * 2 + half
            dest = lax.rem(map_ref[leaf, tile], LEAVES)
            rows = pl.ds(half * BLK, BLK)
            pltpu.make_async_copy(ins[s].at[rows, :], tiles.at[dest], sems.at[dest]).start()
            for pick in range(2):

                @pl.when(dest == group + pick * GROUPS)
                def _():
                    pltpu.make_async_copy(
                        ins[s].at[rows, :],
                        chosen.at[pl.ds(pick * BLK, BLK), :],
                        sems.at[LEAVES + pick],
                    ).start()

    for pick in range(2):
        pltpu.make_async_copy(
            ins[0].at[pl.ds(0, BLK), :],
            chosen.at[pl.ds(pick * BLK, BLK), :],
            sems.at[LEAVES + pick],
        ).wait()
    high[...], low[...] = halves(chosen[...])
    together = 4

    def tile_group(q, _):
        for t in range(together):
            pltpu.make_async_copy(
                ins[0].at[pl.ds(0, BLK), :],
                tiles.at[q * together + t],
                sems.at[q * together + t],
            ).wait()
        rows = tiles[pl.ds(q * together, together)].reshape(together * BLK, S)
        r_high, r_low = halves(rows)
        product = (
            dot_t(r_high, high[...]) + dot_t(r_high, low[...]) + dot_t(r_low, high[...])
        )
        for t in range(together):
            for pick in range(2):
                out[q * together + t, pick] = product[
                    t * BLK : (t + 1) * BLK, pick * BLK : (pick + 1) * BLK
                ]
        return 0

    lax.fori_loop(0, LEAVES // together, tile_group, 0)


def update_blocks(place, child_map, rows):
    return pl.pallas_call(
        update_kernel,
        out_shape=jax.ShapeDtypeStruct((LEAVES, 2, BLK, BLK), F32),
        in_specs=[pl.BlockSpec(memory_space=SMEM)] * 2
        + [pl.BlockSpec(memory_space=pl.ANY)] * GROUPS,
        out_specs=pl.BlockSpec(memory_space=VMEM),
        scratch_shapes=[
            VMEM((LEAVES, BLK, S), F32),
            VMEM((2 * BLK, S), F32),
            VMEM((2 * BLK, S), BF16),
            VMEM((2 * BLK, S), BF16),
            pltpu.SemaphoreType.DMA((LEAVES + 2,)),
        ],
        compiler_params=pltpu.CompilerParams(vmem_limit_bytes=56 * 2**20),
        cost_estimate=pl.CostEstimate(
            flops=8 * 10**9, bytes_accessed=20 * 2**20, transcendentals=0
        ),
    )(place, child_map, *rows)


def assemble_kernel(
    place, map_ref, got, parent, front, column, above, corner, row_level, col_slot
):
    leaf = place[0]
    group = place[1]

    def find(c, _):
        level = jnp.int32(0)
        slots = [jnp.int32(0), jnp.int32(0)]
        for t in range(LEAVES):
            block = map_ref[c, t]
            residue = block & (LEAVES - 1)
            level = jnp.where(residue == leaf, block >> 4, level)
            for pick in range(2):
                slots[pick] = jnp.where(
                    residue == group + pick * GROUPS, block >> 3, slots[pick]
                )
        row_level[c] = level
        for pick in range(2):
            col_slot[c, pick] = slots[pick]
        return 0

    lax.fori_loop(0, LEAVES, find, 0)
    for k in range(8):
        front[k] = parent[pl.ds(k, 4 * BLK, 8), :]

    def subtract(c, _):
        rows = pl.ds(pl.multiple_of(row_level[c] * BLK, BLK), BLK)
        for pick in range(2):
            slot = col_slot[c, pick]
            front[slot, rows, :] = front[slot, rows, :] - got[c, pick]
        return 0

    lax.fori_loop(0, LEAVES, subtract, 0)
    column[...] = front[0]
    above[...] = front[:, :BLK, :]
    corner[...] = front[0, :BLK, :]


def assemble(place, child_map, got, parent):
    return pl.pallas_call(
        assemble_kernel,
        out_shape=(
            jax.ShapeDtypeStruct((8, 4 * BLK, BLK), F32),
            jax.ShapeDtypeStruct((4 * BLK, BLK), F32),
            jax.ShapeDtypeStruct((8, BLK, BLK), F32),
            jax.ShapeDtypeStruct((BLK, BLK), F32),
        ),
        in_specs=[pl.BlockSpec(memory_space=SMEM)] * 2 + [pl.BlockSpec(memory_space=VMEM)] * 2,
        out_specs=(pl.BlockSpec(memory_space=VMEM),) * 4,
        scratch_shapes=[SMEM((LEAVES,), jnp.int32), SMEM((LEAVES, 2), jnp.int32)],
        compiler_params=pltpu.CompilerParams(vmem_limit_bytes=32 * 2**20),
        cost_estimate=pl.CostEstimate(
            flops=10**6, bytes_accessed=6 * 2**20, transcendentals=0
        ),
    )(place, child_map, got, parent)


def panel_kernel(place, here, there, l_ref, inv_ref, block, work):
    leaf = place[0]
    group = place[1]
    for i, ref in enumerate((here, there)):
        for j in range(2):
            for q in range(4):
                rows = pl.ds(pl.multiple_of(((leaf - q) & 3) * BLK, BLK), BLK)
                block[(group & 3) ^ (2 * i + j), rows, :] = ref[j, q * BLK : (q + 1) * BLK]

    def square(r, c):
        rows = slice(r * NB, (r + 1) * NB)
        return jnp.concatenate([block[2 * c, rows, :], block[2 * c + 1, rows, :]], axis=1)

    factor_a, inv_a = diag_block(square(0, 0), work)
    low_left = mul_t(square(1, 0), inv_a)
    factor_b, inv_b = diag_block(square(1, 1) - mul_t(low_left, low_left), work)
    zero = jnp.zeros((NB, NB), F32)
    l_ref[:NB, :NB] = factor_a
    l_ref[:NB, NB:] = zero
    l_ref[NB:, :NB] = low_left
    l_ref[NB:, NB:] = factor_b
    inv_ref[:NB, :NB] = inv_a
    inv_ref[:NB, NB:] = zero
    inv_ref[NB:, :NB] = -mul_n(inv_b, mul_n(low_left, inv_a))
    inv_ref[NB:, NB:] = inv_b


def factor_panel(place, columns):
    return pl.pallas_call(
        panel_kernel,
        out_shape=(jax.ShapeDtypeStruct((PIVOTS, PIVOTS), F32),) * 2,
        in_specs=[pl.BlockSpec(memory_space=SMEM)] + [pl.BlockSpec(memory_space=VMEM)] * 2,
        out_specs=(pl.BlockSpec(memory_space=VMEM),) * 2,
        scratch_shapes=[VMEM((4, PIVOTS, BLK), F32), VMEM((HB, 2 * HB), F32)],
        compiler_params=pltpu.CompilerParams(vmem_limit_bytes=32 * 2**20),
        cost_estimate=pl.CostEstimate(
            flops=25 * 10**9, bytes_accessed=4 * 2**20, transcendentals=0
        ),
    )(place, *columns)


def trailing_kernel(
    place, front, here, there, y0, y1, y2, y3, l_ref, inv_ref, out, panel, above
):
    leaf = place[0]
    group = place[1]
    for i, ref in enumerate((here, there)):
        for j in range(2):
            panel[(group & 3) ^ (2 * i + j)] = ref[j]
    for i, ref in enumerate((y0, y1, y2, y3)):
        above[(leaf - i) & 3] = ref[...]
    inverse = inv_ref[...]
    own = jnp.concatenate([panel[i] for i in range(4)], axis=1)
    solved = mul_t(own, inverse)
    solved_parts = left3(solved)
    inverse_parts = left3(inverse)
    row = lax.broadcasted_iota(jnp.int32, (PIVOTS, BLK), 0)
    in_panel = (row < BLK) & (leaf < 4)
    for pair in range(4):
        across = jnp.concatenate(
            [
                jnp.concatenate([above[q, 2 * pair], above[q, 2 * pair + 1]], axis=1)
                for q in range(4)
            ],
            axis=0,
        )
        across = dot_n(inverse_parts, right3(across, axis=0))
        change = dot_n(solved_parts, right3(across, axis=0))
        for half in range(2):
            k = 2 * pair + half
            value = front[k] - change[:, half * BLK : (half + 1) * BLK]
            out[pl.ds(k, PIVOTS, 8), :] = jnp.where(in_panel, 0.0, value)

    for i in range(4):

        @pl.when(group == i)
        def _():
            out[pl.ds(0, PIVOTS, 8), :] = solved[:, i * BLK : (i + 1) * BLK]

            @pl.when(leaf < 4)
            def _():
                rows = pl.ds(pl.multiple_of((leaf & 3) * BLK, BLK), BLK)
                out[pl.ds(0, BLK, 8), :] = l_ref[rows, i * BLK : (i + 1) * BLK]


def finish(place, front, columns, rows, factor, inverse):
    return pl.pallas_call(
        trailing_kernel,
        out_shape=jax.ShapeDtypeStruct((8 * PIVOTS, BLK), F32),
        in_specs=[pl.BlockSpec(memory_space=SMEM)] + [pl.BlockSpec(memory_space=VMEM)] * 9,
        out_specs=pl.BlockSpec(memory_space=VMEM),
        scratch_shapes=[VMEM((4, PIVOTS, BLK), F32), VMEM((4, 8, BLK, BLK), F32)],
        compiler_params=pltpu.CompilerParams(vmem_limit_bytes=48 * 2**20),
        cost_estimate=pl.CostEstimate(
            flops=5 * 10**9, bytes_accessed=12 * 2**20, transcendentals=0
        ),
    )(place, front, *columns, *rows, factor, inverse)


def group_swap(x, mask, sources=GROUPS):
    return lax.ppermute(x, GROUP, [(a, a ^ mask) for a in range(sources)])


def leaf_column(x, leaf):
    sent = [lax.ppermute(x, "leaf", [(y, 4 * to + y) for y in range(4)]) for to in (1, 2, 3)]
    return jnp.where(leaf < 4, x, sent[0] + sent[1] + sent[2])


def leaf_row(x):
    turned = [
        lax.ppermute(x, "leaf", [(a, (a & 12) | ((a + by) & 3)) for a in range(LEAVES)])
        for by in (1, 2, 3)
    ]
    return [x] + turned


def panel_columns(x, group):
    near = group_swap(x, 1, 4)
    far = group_swap(x, 4, 4)
    across = group_swap(x, 5, 4)
    mine = group < 4
    both = jnp.stack([jnp.where(mine, x, far), jnp.where(mine, near, across)])
    return both, group_swap(both, 2)


def behind(x, earlier):
    return lax.optimization_barrier((x, earlier))[0]


def local(pivot_block, coupling, parent_front, child_map):
    leaf = lax.axis_index("leaf")
    group = lax.axis_index(GROUP)
    place = jnp.stack([leaf, group]).astype(jnp.int32)
    coupled = coupling[0]
    near, across, far = [group_swap(coupled, mask) for mask in (1, 5, 4)]
    factor, factor_own, below, inverses = factor_child(place, pivot_block[0], coupled)
    near, across = solve_rows(factor, inverses, [near, across])
    (far,) = solve_rows(factor, inverses, [far])
    have = {0: below, 1: near, 5: across, 4: far}
    have.update({mask ^ 2: group_swap(x, 2) for mask, x in list(have.items())})
    products = update_blocks(place, child_map, [have[s] for s in range(GROUPS)])
    got = lax.all_to_all(products, "leaf", split_axis=0, concat_axis=0, tiled=True)
    front, column, above, corner = assemble(
        place, child_map, got, parent_front.reshape(8 * PIVOTS, BLK)
    )
    corner = leaf_column(corner, leaf)
    above = leaf_column(behind(above, corner), leaf)
    corner = jnp.concatenate(leaf_row(corner), axis=0)
    corners = panel_columns(corner, group)
    columns = panel_columns(behind(column, corners[0]), group)
    rows = leaf_row(above)
    panel_factor, panel_inverse = factor_panel(place, corners)
    result = finish(place, front, columns, rows, panel_factor, panel_inverse)
    return (
        factor_own[None],
        below[None],
        result.reshape(4, 1, BLK, 8, 1, BLK),
    )


def solution(mesh):
    return jax.shard_map(
        local,
        mesh=mesh,
        in_specs=(
            P("leaf", None, None),
            P("leaf", GROUP, None),
            P(None, "leaf", None, None, GROUP, None),
            P(),
        ),
        out_specs=(
            P("leaf", GROUP, None),
            P("leaf", GROUP, None),
            P(None, "leaf", None, None, GROUP, None),
        ),
        check_vma=False,
    )
```

```python
import functools

import jax
import jax.numpy as jnp
from jax import lax
from jax.experimental import pallas as pl
from jax.experimental.pallas import tpu as pltpu
from jax.sharding import PartitionSpec as P

F32 = jnp.float32
BF16 = jnp.bfloat16
S = 2048
BLK = 128
PIVOTS = 512
LEAVES = 16
GROUPS = 8
NB = 256
HB = 128
SUB = 32
STEPS = S // NB
VMEM = pltpu.VMEM
SMEM = pltpu.SMEM
GROUP = ("row", "col")


def dot_t(a, b):
    return lax.dot_general(a, b, (((1,), (1,)), ((), ())), preferred_element_type=F32)


def dot_n(a, b):
    return lax.dot_general(a, b, (((1,), (0,)), ((), ())), preferred_element_type=F32)


def halves(x):
    high = x.astype(BF16)
    low = (x - high.astype(F32)).astype(BF16)
    return high, low


def left3(x, axis=1):
    high, low = halves(x)
    return jnp.concatenate([high, high, low], axis=axis)


def right3(x, axis=1):
    high, low = halves(x)
    return jnp.concatenate([high, low, high], axis=axis)


def mul_t(a, b):
    return dot_t(left3(a), right3(b))


def mul_n(a, b):
    return dot_n(left3(a), right3(b, axis=0))


def eliminate(rows, base):
    groups = SUB // 8
    sub = lax.broadcasted_iota(jnp.int32, (8, HB), 0)
    state = [
        [rows[8 * a : 8 * a + 8, HB * h : HB * h + HB] for h in range(2)] for a in range(groups)
    ]
    cols = [
        [
            jnp.broadcast_to(rows[8 * a : 8 * a + 8, base + j : base + j + 1], (8, HB))
            if a >= j // 8
            else None
            for a in range(groups)
        ]
        for j in range(SUB)
    ]
    for k in range(SUB):
        own, line = divmod(k, 8)
        inv = lax.rsqrt(jnp.broadcast_to(cols[k][own][line : line + 1, :], (8, HB)))
        scaled = [cols[k][a] * inv if a >= own else None for a in range(groups)]
        below = list(scaled)
        below[own] = jnp.where(sub > line, scaled[own], 0.0)
        for j in range(k + 1, SUB):
            at, spot = divmod(j, 8)
            across = jnp.broadcast_to(scaled[at][spot : spot + 1, :], (8, HB))
            for a in range(at, groups):
                cols[j][a] = cols[j][a] - below[a] * across
        for h in range(2):
            pivot_row = jnp.broadcast_to(state[own][h][line : line + 1, :], (8, HB)) * inv
            state[own][h] = jnp.where(
                sub == line, pivot_row, state[own][h] - below[own] * pivot_row
            )
            for a in range(own + 1, groups):
                state[a][h] = state[a][h] - below[a] * pivot_row
    return jnp.concatenate([jnp.concatenate(pair, axis=1) for pair in state], axis=0)


def diag_small(block, work):
    row = lax.broadcasted_iota(jnp.int32, (HB, HB), 0)
    col = lax.broadcasted_iota(jnp.int32, (HB, HB), 1)
    work[:, :HB] = block
    work[:, HB:] = jnp.where(row == col, 1.0, 0.0)
    for base in range(0, HB, SUB):
        rows = eliminate(work[base : base + SUB, :], base)
        work[base : base + SUB, :] = rows
        after = base + SUB
        if after < HB:
            high = rows.astype(BF16).astype(F32)
            low = rows - high
            left = jnp.concatenate([high[:, :HB], high[:, :HB], low[:, :HB]], axis=0).astype(BF16)
            right = jnp.concatenate([high, low, high], axis=0).astype(BF16)
            product = lax.dot_general(
                left, right, (((0,), (0,)), ((), ())), preferred_element_type=F32
            )
            work[after:, :] = work[after:, :] - product[after:, :]
    return jnp.where(col >= row, work[:, :HB], 0.0), work[:, HB:]


def diag_block(block, work):
    upper_a, inv_a = diag_small(block[:HB, :HB], work)
    low_left = mul_t(block[HB:, :HB], inv_a)
    upper_b, inv_b = diag_small(block[HB:, HB:] - mul_t(low_left, low_left), work)
    inv_low = -mul_n(inv_b, mul_n(low_left, inv_a))
    zero = jnp.zeros((HB, HB), F32)
    factor = jnp.concatenate(
        [
            jnp.concatenate([upper_a.T, zero], axis=1),
            jnp.concatenate([low_left, upper_b.T], axis=1),
        ],
        axis=0,
    )
    inverse = jnp.concatenate(
        [
            jnp.concatenate([inv_a, zero], axis=1),
            jnp.concatenate([inv_low, inv_b], axis=1),
        ],
        axis=0,
    )
    return factor, inverse


def column_place(group, i, j):
    return (group & 3) ^ (2 * i + j) ^ (group >> 2)


def part(i):
    return pl.ds(pl.multiple_of(i * NB, NB), NB)


OWN = STEPS
TALL = 4
TALL_PANEL = 4
ROWS = (OWN + max(TALL, TALL_PANEL)) * NB


def tall(i, count):
    return pl.ds(pl.multiple_of(i * NB, NB), count * NB)


def factor_kernel(
    place, p_hbm, c_hbm, l_hbm, own_hbm, b_hbm, inv_ref, p_vmem, full, work, left, right, sems
):
    def p_copy(i):
        where = (pl.ds(i * NB, NB), pl.ds(0, (i + 1) * NB))
        return pltpu.make_async_copy(p_hbm.at[where], p_vmem.at[where], sems.at[i])

    def l_copy(j):
        where = (pl.ds(j * NB, S - j * NB), pl.ds(j * NB, NB))
        return pltpu.make_async_copy(full.at[where], l_hbm.at[where], sems.at[STEPS + 1 + j])

    c_copy = pltpu.make_async_copy(c_hbm, full.at[pl.ds(S, NB), :], sems.at[STEPS])
    for i in range(STEPS):
        p_copy(i).start()
    c_copy.start()
    for i in range(STEPS):
        p_copy(i).wait()
        rows = slice(i * NB, (i + 1) * NB)
        for k in range(i + 1):
            cols = slice(k * NB, (k + 1) * NB)
            full[rows, cols] = p_vmem[rows, cols].astype(F32)
        if i + 1 < STEPS:
            full[rows, (i + 1) * NB :] = jnp.zeros((NB, S - (i + 1) * NB), F32)
    c_copy.wait()

    def step(j, _):
        factor, inverse = diag_block(full[part(j), part(j)], work)
        full[part(j), part(j)] = factor
        inv_ref[j] = inverse
        inverse_parts = right3(inverse)

        def panel(t, _):
            rows = tall(j + 1 + t * TALL_PANEL, TALL_PANEL)
            x = dot_t(left3(full[rows, part(j)]), inverse_parts)
            full[rows, part(j)] = x
            left[rows, :] = left3(x)
            right[rows, :] = right3(x)
            return 0

        lax.fori_loop(0, (OWN - j + TALL_PANEL - 1) // TALL_PANEL, panel, 0)
        for i in range(STEPS):

            @pl.when(j == i)
            def _():
                l_copy(i).start()

        def trail(k, _):
            def trail_rows(t, _):
                rows = tall(k + t * TALL, TALL)
                full[rows, part(k)] = full[rows, part(k)] - dot_t(left[rows, :], right[part(k), :])
                return 0

            lax.fori_loop(0, (OWN + 1 - k + TALL - 1) // TALL, trail_rows, 0)
            return 0

        lax.fori_loop(j + 1, STEPS, trail, 0)
        return 0

    lax.fori_loop(0, STEPS, step, 0)
    b_copy = pltpu.make_async_copy(full.at[pl.ds(S, NB), :], b_hbm, sems.at[STEPS])
    own_copy = pltpu.make_async_copy(full.at[part(place[1]), :], own_hbm, sems.at[0])
    b_copy.start()
    own_copy.start()
    for j in range(STEPS):
        l_copy(j).wait()
    b_copy.wait()
    own_copy.wait()


def factor_child(place, pivot, coupling):
    return pl.pallas_call(
        factor_kernel,
        out_shape=(
            jax.ShapeDtypeStruct((S, S), F32),
            jax.ShapeDtypeStruct((NB, S), F32),
            jax.ShapeDtypeStruct((NB, S), F32),
            jax.ShapeDtypeStruct((STEPS, NB, NB), F32),
        ),
        in_specs=[pl.BlockSpec(memory_space=SMEM)] + [pl.BlockSpec(memory_space=pl.ANY)] * 2,
        out_specs=(pl.BlockSpec(memory_space=pl.ANY),) * 3 + (pl.BlockSpec(memory_space=VMEM),),
        scratch_shapes=[
            VMEM((S, S), BF16),
            VMEM((ROWS, S), F32),
            VMEM((HB, 2 * HB), F32),
            VMEM((ROWS, 3 * NB), BF16),
            VMEM((ROWS, 3 * NB), BF16),
            pltpu.SemaphoreType.DMA((2 * STEPS + 1,)),
        ],
        compiler_params=pltpu.CompilerParams(vmem_limit_bytes=58 * 2**20),
        cost_estimate=pl.CostEstimate(
            flops=100 * 10**9, bytes_accessed=30 * 2**20, transcendentals=0
        ),
    )(place, pivot, coupling)


def solve_kernel(count, after, l_hbm, inv_ref, *refs):
    ins = refs[:count]
    outs = refs[count + after : 2 * count + after]
    l_vmem, c_vmem, parts, sems = refs[2 * count + after :]

    def l_copy(j):
        where = (pl.ds(j * NB, NB), pl.ds(0, (j + 1) * NB))
        return pltpu.make_async_copy(l_hbm.at[where], l_vmem.at[where], sems.at[j])

    def c_copy(j, i):
        cols = pl.ds(j * NB, NB)
        return pltpu.make_async_copy(
            ins[i].at[:, cols], c_vmem.at[pl.ds(i * NB, NB), cols], sems.at[STEPS + j * count + i]
        )

    for j in range(STEPS):
        l_copy(j).start()
        for i in range(count):
            c_copy(j, i).start()
    for j in range(STEPS):
        l_copy(j).wait()
        for i in range(count):
            c_copy(j, i).wait()
        rhs = c_vmem[:, j * NB : (j + 1) * NB]
        if j:
            strip = jnp.concatenate(
                [
                    right3(l_vmem[j * NB : (j + 1) * NB, k * NB : (k + 1) * NB])
                    for k in range(j)
                ],
                axis=1,
            )
            newest = 3 * (j - 1) * NB
            if newest:
                rhs = rhs - dot_t(parts[:, :newest], strip[:, :newest])
            rhs = rhs - dot_t(parts[:, newest : newest + 3 * NB], strip[:, newest:])
        x = mul_t(rhs, inv_ref[j])
        if j + 1 < STEPS:
            parts[:, 3 * j * NB : 3 * (j + 1) * NB] = left3(x)
        for i in range(count):
            outs[i][:, j * NB : (j + 1) * NB] = x[i * NB : (i + 1) * NB]


def solve_rows(factor, inverses, rows, after=()):
    count = len(rows)
    return pl.pallas_call(
        functools.partial(solve_kernel, count, len(after)),
        out_shape=(jax.ShapeDtypeStruct((NB, S), F32),) * count,
        in_specs=[pl.BlockSpec(memory_space=pl.ANY), pl.BlockSpec(memory_space=VMEM)]
        + [pl.BlockSpec(memory_space=pl.ANY)] * (count + len(after)),
        out_specs=(pl.BlockSpec(memory_space=VMEM),) * count,
        scratch_shapes=[
            VMEM((S, S), F32),
            VMEM((count * NB, S), F32),
            VMEM((count * NB, 3 * (S - NB)), BF16),
            pltpu.SemaphoreType.DMA((STEPS * (1 + count),)),
        ],
        compiler_params=pltpu.CompilerParams(vmem_limit_bytes=56 * 2**20),
        cost_estimate=pl.CostEstimate(
            flops=count * 7 * 10**9, bytes_accessed=24 * 2**20, transcendentals=0
        ),
    )(factor, inverses, *rows, *after)


def update_kernel(place, map_ref, *refs):
    ins = refs[:GROUPS]
    out, tiles, chosen, high, low, sems = refs[GROUPS:]
    leaf = place[0]
    group = place[1]
    for s in range(GROUPS):
        for half in range(2):
            tile = (group ^ s) * 2 + half
            dest = lax.rem(map_ref[leaf, tile], LEAVES)
            rows = pl.ds(half * BLK, BLK)
            pltpu.make_async_copy(ins[s].at[rows, :], tiles.at[dest], sems.at[dest]).start()
            for pick in range(2):

                @pl.when(dest == group + pick * GROUPS)
                def _():
                    pltpu.make_async_copy(
                        ins[s].at[rows, :],
                        chosen.at[pl.ds(pick * BLK, BLK), :],
                        sems.at[LEAVES + pick],
                    ).start()

    for pick in range(2):
        pltpu.make_async_copy(
            ins[0].at[pl.ds(0, BLK), :],
            chosen.at[pl.ds(pick * BLK, BLK), :],
            sems.at[LEAVES + pick],
        ).wait()
    high[...], low[...] = halves(chosen[...])
    together = 4

    def tile_group(q, _):
        for t in range(together):
            pltpu.make_async_copy(
                ins[0].at[pl.ds(0, BLK), :],
                tiles.at[q * together + t],
                sems.at[q * together + t],
            ).wait()
        rows = tiles[pl.ds(q * together, together)].reshape(together * BLK, S)
        r_high, r_low = halves(rows)
        product = (
            dot_t(r_high, high[...]) + dot_t(r_high, low[...]) + dot_t(r_low, high[...])
        )
        for t in range(together):
            for pick in range(2):
                out[q * together + t, pick] = product[
                    t * BLK : (t + 1) * BLK, pick * BLK : (pick + 1) * BLK
                ]
        return 0

    lax.fori_loop(0, LEAVES // together, tile_group, 0)


def update_blocks(place, child_map, rows):
    return pl.pallas_call(
        update_kernel,
        out_shape=jax.ShapeDtypeStruct((LEAVES, 2, BLK, BLK), F32),
        in_specs=[pl.BlockSpec(memory_space=SMEM)] * 2
        + [pl.BlockSpec(memory_space=pl.ANY)] * GROUPS,
        out_specs=pl.BlockSpec(memory_space=VMEM),
        scratch_shapes=[
            VMEM((LEAVES, BLK, S), F32),
            VMEM((2 * BLK, S), F32),
            VMEM((2 * BLK, S), BF16),
            VMEM((2 * BLK, S), BF16),
            pltpu.SemaphoreType.DMA((LEAVES + 2,)),
        ],
        compiler_params=pltpu.CompilerParams(vmem_limit_bytes=56 * 2**20),
        cost_estimate=pl.CostEstimate(
            flops=8 * 10**9, bytes_accessed=20 * 2**20, transcendentals=0
        ),
    )(place, child_map, *rows)


def assemble_kernel(
    place, map_ref, got, parent, front, column, above, corner, row_level, col_slot
):
    leaf = place[0]
    group = place[1]

    def find(c, _):
        level = jnp.int32(0)
        slots = [jnp.int32(0), jnp.int32(0)]
        for t in range(LEAVES):
            block = map_ref[c, t]
            residue = block & (LEAVES - 1)
            level = jnp.where(residue == leaf, block >> 4, level)
            for pick in range(2):
                slots[pick] = jnp.where(
                    residue == group + pick * GROUPS, block >> 3, slots[pick]
                )
        row_level[c] = level
        for pick in range(2):
            col_slot[c, pick] = slots[pick]
        return 0

    lax.fori_loop(0, LEAVES, find, 0)
    for k in range(8):
        front[k] = parent[pl.ds(k, 4 * BLK, 8), :]

    def subtract(c, _):
        rows = pl.ds(pl.multiple_of(row_level[c] * BLK, BLK), BLK)
        for pick in range(2):
            slot = col_slot[c, pick]
            front[slot, rows, :] = front[slot, rows, :] - got[c, pick]
        return 0

    lax.fori_loop(0, LEAVES, subtract, 0)
    column[...] = front[0]
    above[...] = front[:, :BLK, :]
    corner[...] = front[0, :BLK, :]


def assemble(place, child_map, got, parent):
    return pl.pallas_call(
        assemble_kernel,
        out_shape=(
            jax.ShapeDtypeStruct((8, 4 * BLK, BLK), F32),
            jax.ShapeDtypeStruct((4 * BLK, BLK), F32),
            jax.ShapeDtypeStruct((8, BLK, BLK), F32),
            jax.ShapeDtypeStruct((BLK, BLK), F32),
        ),
        in_specs=[pl.BlockSpec(memory_space=SMEM)] * 2 + [pl.BlockSpec(memory_space=VMEM)] * 2,
        out_specs=(pl.BlockSpec(memory_space=VMEM),) * 4,
        scratch_shapes=[SMEM((LEAVES,), jnp.int32), SMEM((LEAVES, 2), jnp.int32)],
        compiler_params=pltpu.CompilerParams(vmem_limit_bytes=32 * 2**20),
        cost_estimate=pl.CostEstimate(
            flops=10**6, bytes_accessed=6 * 2**20, transcendentals=0
        ),
    )(place, child_map, got, parent)


def panel_kernel(place, here, there, l_ref, inv_ref, block, work):
    leaf = place[0]
    group = place[1]
    for i, ref in enumerate((here, there)):
        for j in range(2):
            for q in range(4):
                rows = pl.ds(pl.multiple_of(((leaf - q) & 3) * BLK, BLK), BLK)
                block[column_place(group, i, j), rows, :] = ref[j, q * BLK : (q + 1) * BLK]

    def square(r, c):
        rows = slice(r * NB, (r + 1) * NB)
        return jnp.concatenate([block[2 * c, rows, :], block[2 * c + 1, rows, :]], axis=1)

    factor_a, inv_a = diag_block(square(0, 0), work)
    low_left = mul_t(square(1, 0), inv_a)
    factor_b, inv_b = diag_block(square(1, 1) - mul_t(low_left, low_left), work)
    zero = jnp.zeros((NB, NB), F32)
    l_ref[:NB, :NB] = factor_a
    l_ref[:NB, NB:] = zero
    l_ref[NB:, :NB] = low_left
    l_ref[NB:, NB:] = factor_b
    inv_ref[:NB, :NB] = inv_a
    inv_ref[:NB, NB:] = zero
    inv_ref[NB:, :NB] = -mul_n(inv_b, mul_n(low_left, inv_a))
    inv_ref[NB:, NB:] = inv_b


def factor_panel(place, columns):
    return pl.pallas_call(
        panel_kernel,
        out_shape=(jax.ShapeDtypeStruct((PIVOTS, PIVOTS), F32),) * 2,
        in_specs=[pl.BlockSpec(memory_space=SMEM)] + [pl.BlockSpec(memory_space=VMEM)] * 2,
        out_specs=(pl.BlockSpec(memory_space=VMEM),) * 2,
        scratch_shapes=[VMEM((4, PIVOTS, BLK), F32), VMEM((HB, 2 * HB), F32)],
        compiler_params=pltpu.CompilerParams(vmem_limit_bytes=32 * 2**20),
        cost_estimate=pl.CostEstimate(
            flops=25 * 10**9, bytes_accessed=4 * 2**20, transcendentals=0
        ),
    )(place, *columns)


def trailing_kernel(
    place, front, here, there, y0, y1, y2, y3, l_ref, inv_ref, out, panel, above
):
    leaf = place[0]
    group = place[1]
    for i, ref in enumerate((here, there)):
        for j in range(2):
            panel[column_place(group, i, j)] = ref[j]
    for i, ref in enumerate((y0, y1, y2, y3)):
        above[(leaf - i) & 3] = ref[...]
    inverse = inv_ref[...]
    own = jnp.concatenate([panel[i] for i in range(4)], axis=1)
    solved = mul_t(own, inverse)
    solved_parts = left3(solved)
    inverse_parts = left3(inverse)
    row = lax.broadcasted_iota(jnp.int32, (PIVOTS, BLK), 0)
    in_panel = (row < BLK) & (leaf < 4)
    for pair in range(4):
        across = jnp.concatenate(
            [
                jnp.concatenate([above[q, 2 * pair], above[q, 2 * pair + 1]], axis=1)
                for q in range(4)
            ],
            axis=0,
        )
        across = dot_n(inverse_parts, right3(across, axis=0))
        change = dot_n(solved_parts, right3(across, axis=0))
        for half in range(2):
            k = 2 * pair + half
            value = front[k] - change[:, half * BLK : (half + 1) * BLK]
            out[pl.ds(k, PIVOTS, 8), :] = jnp.where(in_panel, 0.0, value)

    for i in range(4):

        @pl.when(group == i)
        def _():
            out[pl.ds(0, PIVOTS, 8), :] = solved[:, i * BLK : (i + 1) * BLK]

            @pl.when(leaf < 4)
            def _():
                rows = pl.ds(pl.multiple_of((leaf & 3) * BLK, BLK), BLK)
                out[pl.ds(0, BLK, 8), :] = l_ref[rows, i * BLK : (i + 1) * BLK]


def finish(place, front, columns, rows, factor, inverse):
    return pl.pallas_call(
        trailing_kernel,
        out_shape=jax.ShapeDtypeStruct((8 * PIVOTS, BLK), F32),
        in_specs=[pl.BlockSpec(memory_space=SMEM)] + [pl.BlockSpec(memory_space=VMEM)] * 9,
        out_specs=pl.BlockSpec(memory_space=VMEM),
        scratch_shapes=[VMEM((4, PIVOTS, BLK), F32), VMEM((4, 8, BLK, BLK), F32)],
        compiler_params=pltpu.CompilerParams(vmem_limit_bytes=48 * 2**20),
        cost_estimate=pl.CostEstimate(
            flops=5 * 10**9, bytes_accessed=12 * 2**20, transcendentals=0
        ),
    )(place, front, *columns, *rows, factor, inverse)


def group_swap(x, mask, sources=GROUPS):
    return lax.ppermute(x, GROUP, [(a, a ^ mask) for a in range(sources)])


def leaf_column(x, leaf):
    sent = [lax.ppermute(x, "leaf", [(y, 4 * to + y) for y in range(4)]) for to in (1, 2, 3)]
    return jnp.where(leaf < 4, x, sent[0] + sent[1] + sent[2])


def leaf_row(x):
    turned = [
        lax.ppermute(x, "leaf", [(a, (a & 12) | ((a + by) & 3)) for a in range(LEAVES)])
        for by in (1, 2, 3)
    ]
    return [x] + turned


def panel_columns(x, group):
    have = jnp.where(group < 4, x, group_swap(x, 5, 4))
    both = jnp.stack([have, group_swap(have, 1)])
    return both, group_swap(both, 2)


def behind(x, earlier):
    return lax.optimization_barrier((x, earlier))[0]


def local(pivot_block, coupling, parent_front, child_map):
    leaf = lax.axis_index("leaf")
    group = lax.axis_index(GROUP)
    place = jnp.stack([leaf, group]).astype(jnp.int32)
    coupled = coupling[0]
    near, across, far = [group_swap(coupled, mask) for mask in (1, 5, 4)]
    factor, factor_own, below, inverses = factor_child(place, pivot_block[0], coupled)
    near, across = solve_rows(factor, inverses, [near, across])
    (far,) = solve_rows(factor, inverses, [far])
    have = {0: below, 1: near, 5: across, 4: far}
    have.update({mask ^ 2: group_swap(x, 2) for mask, x in list(have.items())})
    products = update_blocks(place, child_map, [have[s] for s in range(GROUPS)])
    got = lax.all_to_all(products, "leaf", split_axis=0, concat_axis=0, tiled=True)
    front, column, above, corner = assemble(
        place, child_map, got, parent_front.reshape(8 * PIVOTS, BLK)
    )
    corner = leaf_column(corner, leaf)
    above = leaf_column(behind(above, corner), leaf)
    corner = jnp.concatenate(leaf_row(corner), axis=0)
    corners = panel_columns(corner, group)
    columns = panel_columns(behind(column, corners[0]), group)
    rows = leaf_row(above)
    panel_factor, panel_inverse = factor_panel(place, corners)
    result = finish(place, front, columns, rows, panel_factor, panel_inverse)
    return (
        factor_own[None],
        below[None],
        result.reshape(4, 1, BLK, 8, 1, BLK),
    )


def solution(mesh):
    return jax.shard_map(
        local,
        mesh=mesh,
        in_specs=(
            P("leaf", None, None),
            P("leaf", GROUP, None),
            P(None, "leaf", None, None, GROUP, None),
            P(),
        ),
        out_specs=(
            P("leaf", GROUP, None),
            P("leaf", GROUP, None),
            P(None, "leaf", None, None, GROUP, None),
        ),
        check_vma=False,
    )
```

```python
import functools

import jax
import jax.numpy as jnp
from jax import lax
from jax.experimental import pallas as pl
from jax.experimental.pallas import tpu as pltpu
from jax.sharding import PartitionSpec as P

F32 = jnp.float32
BF16 = jnp.bfloat16
S = 2048
BLK = 128
PIVOTS = 512
LEAVES = 16
GROUPS = 8
NB = 256
HB = 128
SUB = 32
STEPS = S // NB
VMEM = pltpu.VMEM
SMEM = pltpu.SMEM
GROUP = ("row", "col")


def dot_t(a, b):
    return lax.dot_general(a, b, (((1,), (1,)), ((), ())), preferred_element_type=F32)


def dot_n(a, b):
    return lax.dot_general(a, b, (((1,), (0,)), ((), ())), preferred_element_type=F32)


def halves(x):
    high = x.astype(BF16)
    low = (x - high.astype(F32)).astype(BF16)
    return high, low


def left3(x, axis=1):
    high, low = halves(x)
    return jnp.concatenate([high, high, low], axis=axis)


def right3(x, axis=1):
    high, low = halves(x)
    return jnp.concatenate([high, low, high], axis=axis)


def mul_t(a, b):
    return dot_t(left3(a), right3(b))


def mul_n(a, b):
    return dot_n(left3(a), right3(b, axis=0))


def eliminate(rows, base):
    groups = SUB // 8
    sub = lax.broadcasted_iota(jnp.int32, (8, HB), 0)
    state = [
        [rows[8 * a : 8 * a + 8, HB * h : HB * h + HB] for h in range(2)] for a in range(groups)
    ]
    cols = [
        [
            jnp.broadcast_to(rows[8 * a : 8 * a + 8, base + j : base + j + 1], (8, HB))
            if a >= j // 8
            else None
            for a in range(groups)
        ]
        for j in range(SUB)
    ]
    for k in range(SUB):
        own, line = divmod(k, 8)
        inv = lax.rsqrt(jnp.broadcast_to(cols[k][own][line : line + 1, :], (8, HB)))
        scaled = [cols[k][a] * inv if a >= own else None for a in range(groups)]
        below = list(scaled)
        below[own] = jnp.where(sub > line, scaled[own], 0.0)
        for j in range(k + 1, SUB):
            at, spot = divmod(j, 8)
            across = jnp.broadcast_to(scaled[at][spot : spot + 1, :], (8, HB))
            for a in range(at, groups):
                cols[j][a] = cols[j][a] - below[a] * across
        for h in range(2):
            pivot_row = jnp.broadcast_to(state[own][h][line : line + 1, :], (8, HB)) * inv
            state[own][h] = jnp.where(
                sub == line, pivot_row, state[own][h] - below[own] * pivot_row
            )
            for a in range(own + 1, groups):
                state[a][h] = state[a][h] - below[a] * pivot_row
    return jnp.concatenate([jnp.concatenate(pair, axis=1) for pair in state], axis=0)


def diag_small(block, work):
    row = lax.broadcasted_iota(jnp.int32, (HB, HB), 0)
    col = lax.broadcasted_iota(jnp.int32, (HB, HB), 1)
    work[:, :HB] = block
    work[:, HB:] = jnp.where(row == col, 1.0, 0.0)
    for base in range(0, HB, SUB):
        rows = eliminate(work[base : base + SUB, :], base)
        work[base : base + SUB, :] = rows
        after = base + SUB
        if after < HB:
            high = rows.astype(BF16).astype(F32)
            low = rows - high
            left = jnp.concatenate([high[:, :HB], high[:, :HB], low[:, :HB]], axis=0).astype(BF16)
            right = jnp.concatenate([high, low, high], axis=0).astype(BF16)
            product = lax.dot_general(
                left, right, (((0,), (0,)), ((), ())), preferred_element_type=F32
            )
            work[after:, :] = work[after:, :] - product[after:, :]
    return jnp.where(col >= row, work[:, :HB], 0.0), work[:, HB:]


def diag_block(block, work):
    upper_a, inv_a = diag_small(block[:HB, :HB], work)
    low_left = mul_t(block[HB:, :HB], inv_a)
    upper_b, inv_b = diag_small(block[HB:, HB:] - mul_t(low_left, low_left), work)
    inv_low = -mul_n(inv_b, mul_n(low_left, inv_a))
    zero = jnp.zeros((HB, HB), F32)
    factor = jnp.concatenate(
        [
            jnp.concatenate([upper_a.T, zero], axis=1),
            jnp.concatenate([low_left, upper_b.T], axis=1),
        ],
        axis=0,
    )
    inverse = jnp.concatenate(
        [
            jnp.concatenate([inv_a, zero], axis=1),
            jnp.concatenate([inv_low, inv_b], axis=1),
        ],
        axis=0,
    )
    return factor, inverse


def column_place(group, i, j):
    return (group & 3) ^ (2 * i + j) ^ (group >> 2)


def part(i):
    return pl.ds(pl.multiple_of(i * NB, NB), NB)


OWN = STEPS
TALL = 4
TALL_PANEL = 4
ROWS = (OWN + max(TALL, TALL_PANEL)) * NB


def tall(i, count):
    return pl.ds(pl.multiple_of(i * NB, NB), count * NB)


def factor_kernel(
    place, p_hbm, c_hbm, l_hbm, own_hbm, b_hbm, inv_ref, p_vmem, full, work, left, right, sems
):
    def p_copy(i):
        where = (pl.ds(i * NB, NB), pl.ds(0, (i + 1) * NB))
        return pltpu.make_async_copy(p_hbm.at[where], p_vmem.at[where], sems.at[i])

    def l_copy(j):
        where = (pl.ds(j * NB, S - j * NB), pl.ds(j * NB, NB))
        return pltpu.make_async_copy(full.at[where], l_hbm.at[where], sems.at[STEPS + 1 + j])

    c_copy = pltpu.make_async_copy(c_hbm, full.at[pl.ds(S, NB), :], sems.at[STEPS])
    def b_copy(j):
        cols = pl.ds(j * NB, NB)
        return pltpu.make_async_copy(
            full.at[pl.ds(S, NB), cols], b_hbm.at[:, cols], sems.at[2 * STEPS + 1 + j]
        )

    own_copy = pltpu.make_async_copy(
        full.at[part(place[1]), :], own_hbm, sems.at[3 * STEPS + 1]
    )
    for i in range(STEPS):
        p_copy(i).start()
    c_copy.start()

    def load_row(i):
        p_copy(i).wait()
        rows = slice(i * NB, (i + 1) * NB)
        for k in range(i + 1):
            cols = slice(k * NB, (k + 1) * NB)
            full[rows, cols] = p_vmem[rows, cols].astype(F32)
        if i + 1 < STEPS:
            full[rows, (i + 1) * NB :] = jnp.zeros((NB, S - (i + 1) * NB), F32)

    load_row(0)

    def step(j, _):
        factor, inverse = diag_block(full[part(j), part(j)], work)
        full[part(j), part(j)] = factor
        inv_ref[j] = inverse
        inverse_parts = right3(inverse)

        @pl.when(j == 0)
        def _():
            for i in range(1, STEPS):
                load_row(i)
            c_copy.wait()

        def panel(t, _):
            rows = tall(j + 1 + t * TALL_PANEL, TALL_PANEL)
            x = dot_t(left3(full[rows, part(j)]), inverse_parts)
            full[rows, part(j)] = x
            left[rows, :] = left3(x)
            right[rows, :] = right3(x)
            return 0

        lax.fori_loop(0, (OWN - j + TALL_PANEL - 1) // TALL_PANEL, panel, 0)
        for i in range(STEPS):

            @pl.when(j == i)
            def _():
                l_copy(i).start()
                b_copy(i).start()

        @pl.when(j == place[1])
        def _():
            own_copy.start()

        def trail(k, _):
            def trail_rows(t, _):
                rows = tall(k + t * TALL, TALL)
                full[rows, part(k)] = full[rows, part(k)] - dot_t(left[rows, :], right[part(k), :])
                return 0

            lax.fori_loop(0, (OWN + 1 - k + TALL - 1) // TALL, trail_rows, 0)
            return 0

        lax.fori_loop(j + 1, STEPS, trail, 0)
        return 0

    lax.fori_loop(0, STEPS, step, 0)
    for j in range(STEPS):
        l_copy(j).wait()
        b_copy(j).wait()
    own_copy.wait()


def factor_child(place, pivot, coupling):
    return pl.pallas_call(
        factor_kernel,
        out_shape=(
            jax.ShapeDtypeStruct((S, S), F32),
            jax.ShapeDtypeStruct((NB, S), F32),
            jax.ShapeDtypeStruct((NB, S), F32),
            jax.ShapeDtypeStruct((STEPS, NB, NB), F32),
        ),
        in_specs=[pl.BlockSpec(memory_space=SMEM)] + [pl.BlockSpec(memory_space=pl.ANY)] * 2,
        out_specs=(pl.BlockSpec(memory_space=pl.ANY),) * 3 + (pl.BlockSpec(memory_space=VMEM),),
        scratch_shapes=[
            VMEM((S, S), BF16),
            VMEM((ROWS, S), F32),
            VMEM((HB, 2 * HB), F32),
            VMEM((ROWS, 3 * NB), BF16),
            VMEM((ROWS, 3 * NB), BF16),
            pltpu.SemaphoreType.DMA((3 * STEPS + 2,)),
        ],
        compiler_params=pltpu.CompilerParams(vmem_limit_bytes=52 * 2**20),
        cost_estimate=pl.CostEstimate(
            flops=100 * 10**9, bytes_accessed=30 * 2**20, transcendentals=0
        ),
    )(place, pivot, coupling)


def solve_kernel(count, after, l_hbm, inv_ref, *refs):
    ins = refs[:count]
    outs = refs[count + after : 2 * count + after]
    l_vmem, c_vmem, parts, sems = refs[2 * count + after :]

    def l_copy(j):
        where = (pl.ds(j * NB, NB), pl.ds(0, (j + 1) * NB))
        return pltpu.make_async_copy(l_hbm.at[where], l_vmem.at[where], sems.at[j])

    def c_copy(j, i):
        cols = pl.ds(j * NB, NB)
        return pltpu.make_async_copy(
            ins[i].at[:, cols], c_vmem.at[pl.ds(i * NB, NB), cols], sems.at[STEPS + j * count + i]
        )

    for j in range(STEPS):
        l_copy(j).start()
        for i in range(count):
            c_copy(j, i).start()
    for j in range(STEPS):
        l_copy(j).wait()
        for i in range(count):
            c_copy(j, i).wait()
        rhs = c_vmem[:, j * NB : (j + 1) * NB]
        if j:
            strip = jnp.concatenate(
                [
                    right3(l_vmem[j * NB : (j + 1) * NB, k * NB : (k + 1) * NB])
                    for k in range(j)
                ],
                axis=1,
            )
            newest = 3 * (j - 1) * NB
            if newest:
                rhs = rhs - dot_t(parts[:, :newest], strip[:, :newest])
            rhs = rhs - dot_t(parts[:, newest : newest + 3 * NB], strip[:, newest:])
        x = mul_t(rhs, inv_ref[j])
        if j + 1 < STEPS:
            parts[:, 3 * j * NB : 3 * (j + 1) * NB] = left3(x)
        for i in range(count):
            outs[i][:, j * NB : (j + 1) * NB] = x[i * NB : (i + 1) * NB]


def solve_rows(factor, inverses, rows, after=()):
    count = len(rows)
    return pl.pallas_call(
        functools.partial(solve_kernel, count, len(after)),
        out_shape=(jax.ShapeDtypeStruct((NB, S), F32),) * count,
        in_specs=[pl.BlockSpec(memory_space=pl.ANY), pl.BlockSpec(memory_space=VMEM)]
        + [pl.BlockSpec(memory_space=pl.ANY)] * (count + len(after)),
        out_specs=(pl.BlockSpec(memory_space=VMEM),) * count,
        scratch_shapes=[
            VMEM((S, S), F32),
            VMEM((count * NB, S), F32),
            VMEM((count * NB, 3 * (S - NB)), BF16),
            pltpu.SemaphoreType.DMA((STEPS * (1 + count),)),
        ],
        compiler_params=pltpu.CompilerParams(vmem_limit_bytes=(24 + 10 * count) * 2**20),
        cost_estimate=pl.CostEstimate(
            flops=count * 7 * 10**9, bytes_accessed=24 * 2**20, transcendentals=0
        ),
    )(factor, inverses, *rows, *after)


def update_kernel(place, map_ref, *refs):
    ins = refs[:GROUPS]
    out, tiles, chosen, high, low, sems = refs[GROUPS:]
    leaf = place[0]
    group = place[1]
    for s in range(GROUPS):
        for half in range(2):
            tile = (group ^ s) * 2 + half
            dest = lax.rem(map_ref[leaf, tile], LEAVES)
            rows = pl.ds(half * BLK, BLK)
            pltpu.make_async_copy(ins[s].at[rows, :], tiles.at[dest], sems.at[dest]).start()
            for pick in range(2):

                @pl.when(dest == group + pick * GROUPS)
                def _():
                    pltpu.make_async_copy(
                        ins[s].at[rows, :],
                        chosen.at[pl.ds(pick * BLK, BLK), :],
                        sems.at[LEAVES + pick],
                    ).start()

    for pick in range(2):
        pltpu.make_async_copy(
            ins[0].at[pl.ds(0, BLK), :],
            chosen.at[pl.ds(pick * BLK, BLK), :],
            sems.at[LEAVES + pick],
        ).wait()
    high[...], low[...] = halves(chosen[...])
    together = 4

    def tile_group(q, _):
        for t in range(together):
            pltpu.make_async_copy(
                ins[0].at[pl.ds(0, BLK), :],
                tiles.at[q * together + t],
                sems.at[q * together + t],
            ).wait()
        rows = tiles[pl.ds(q * together, together)].reshape(together * BLK, S)
        r_high, r_low = halves(rows)
        product = (
            dot_t(r_high, high[...]) + dot_t(r_high, low[...]) + dot_t(r_low, high[...])
        )
        for t in range(together):
            for pick in range(2):
                out[q * together + t, pick] = product[
                    t * BLK : (t + 1) * BLK, pick * BLK : (pick + 1) * BLK
                ]
        return 0

    lax.fori_loop(0, LEAVES // together, tile_group, 0)


def update_blocks(place, child_map, rows):
    return pl.pallas_call(
        update_kernel,
        out_shape=jax.ShapeDtypeStruct((LEAVES, 2, BLK, BLK), F32),
        in_specs=[pl.BlockSpec(memory_space=SMEM)] * 2
        + [pl.BlockSpec(memory_space=pl.ANY)] * GROUPS,
        out_specs=pl.BlockSpec(memory_space=VMEM),
        scratch_shapes=[
            VMEM((LEAVES, BLK, S), F32),
            VMEM((2 * BLK, S), F32),
            VMEM((2 * BLK, S), BF16),
            VMEM((2 * BLK, S), BF16),
            pltpu.SemaphoreType.DMA((LEAVES + 2,)),
        ],
        compiler_params=pltpu.CompilerParams(vmem_limit_bytes=33 * 2**20),
        cost_estimate=pl.CostEstimate(
            flops=8 * 10**9, bytes_accessed=20 * 2**20, transcendentals=0
        ),
    )(place, child_map, *rows)


def assemble_kernel(
    place, map_ref, got, parent, front, column, above, corner, row_level, col_slot
):
    leaf = place[0]
    group = place[1]

    def find(c, _):
        level = jnp.int32(0)
        slots = [jnp.int32(0), jnp.int32(0)]
        for t in range(LEAVES):
            block = map_ref[c, t]
            residue = block & (LEAVES - 1)
            level = jnp.where(residue == leaf, block >> 4, level)
            for pick in range(2):
                slots[pick] = jnp.where(
                    residue == group + pick * GROUPS, block >> 3, slots[pick]
                )
        row_level[c] = level
        for pick in range(2):
            col_slot[c, pick] = slots[pick]
        return 0

    lax.fori_loop(0, LEAVES, find, 0)
    for k in range(8):
        front[k] = parent[pl.ds(k, 4 * BLK, 8), :]

    def subtract(c, _):
        rows = pl.ds(pl.multiple_of(row_level[c] * BLK, BLK), BLK)
        for pick in range(2):
            slot = col_slot[c, pick]
            front[slot, rows, :] = front[slot, rows, :] - got[c, pick]
        return 0

    lax.fori_loop(0, LEAVES, subtract, 0)
    column[...] = front[0]
    above[...] = front[:, :BLK, :]
    corner[...] = front[0, :BLK, :]


def assemble(place, child_map, got, parent):
    return pl.pallas_call(
        assemble_kernel,
        out_shape=(
            jax.ShapeDtypeStruct((8, 4 * BLK, BLK), F32),
            jax.ShapeDtypeStruct((4 * BLK, BLK), F32),
            jax.ShapeDtypeStruct((8, BLK, BLK), F32),
            jax.ShapeDtypeStruct((BLK, BLK), F32),
        ),
        in_specs=[pl.BlockSpec(memory_space=SMEM)] * 2 + [pl.BlockSpec(memory_space=VMEM)] * 2,
        out_specs=(pl.BlockSpec(memory_space=VMEM),) * 4,
        scratch_shapes=[SMEM((LEAVES,), jnp.int32), SMEM((LEAVES, 2), jnp.int32)],
        compiler_params=pltpu.CompilerParams(vmem_limit_bytes=16 * 2**20),
        cost_estimate=pl.CostEstimate(
            flops=10**6, bytes_accessed=6 * 2**20, transcendentals=0
        ),
    )(place, child_map, got, parent)


def panel_kernel(place, here, there, l_ref, inv_ref, block, work):
    leaf = place[0]
    group = place[1]
    for i, ref in enumerate((here, there)):
        for j in range(2):
            for q in range(4):
                rows = pl.ds(pl.multiple_of(((leaf - q) & 3) * BLK, BLK), BLK)
                block[column_place(group, i, j), rows, :] = ref[j, q * BLK : (q + 1) * BLK]

    def square(r, c):
        rows = slice(r * NB, (r + 1) * NB)
        return jnp.concatenate([block[2 * c, rows, :], block[2 * c + 1, rows, :]], axis=1)

    factor_a, inv_a = diag_block(square(0, 0), work)
    low_left = mul_t(square(1, 0), inv_a)
    factor_b, inv_b = diag_block(square(1, 1) - mul_t(low_left, low_left), work)
    zero = jnp.zeros((NB, NB), F32)
    l_ref[:NB, :NB] = factor_a
    l_ref[:NB, NB:] = zero
    l_ref[NB:, :NB] = low_left
    l_ref[NB:, NB:] = factor_b
    inv_ref[:NB, :NB] = inv_a
    inv_ref[:NB, NB:] = zero
    inv_ref[NB:, :NB] = -mul_n(inv_b, mul_n(low_left, inv_a))
    inv_ref[NB:, NB:] = inv_b


def factor_panel(place, columns):
    return pl.pallas_call(
        panel_kernel,
        out_shape=(jax.ShapeDtypeStruct((PIVOTS, PIVOTS), F32),) * 2,
        in_specs=[pl.BlockSpec(memory_space=SMEM)] + [pl.BlockSpec(memory_space=VMEM)] * 2,
        out_specs=(pl.BlockSpec(memory_space=VMEM),) * 2,
        scratch_shapes=[VMEM((4, PIVOTS, BLK), F32), VMEM((HB, 2 * HB), F32)],
        compiler_params=pltpu.CompilerParams(vmem_limit_bytes=16 * 2**20),
        cost_estimate=pl.CostEstimate(
            flops=25 * 10**9, bytes_accessed=4 * 2**20, transcendentals=0
        ),
    )(place, *columns)


def trailing_kernel(
    place, front, here, there, y0, y1, y2, y3, l_ref, inv_ref, out, panel, above
):
    leaf = place[0]
    group = place[1]
    for i, ref in enumerate((here, there)):
        for j in range(2):
            panel[column_place(group, i, j)] = ref[j]
    for i, ref in enumerate((y0, y1, y2, y3)):
        above[(leaf - i) & 3] = ref[...]
    inverse = inv_ref[...]
    own = jnp.concatenate([panel[i] for i in range(4)], axis=1)
    solved = mul_t(own, inverse)
    solved_parts = left3(solved)
    inverse_parts = left3(inverse)
    row = lax.broadcasted_iota(jnp.int32, (PIVOTS, BLK), 0)
    in_panel = (row < BLK) & (leaf < 4)
    for pair in range(4):
        across = jnp.concatenate(
            [
                jnp.concatenate([above[q, 2 * pair], above[q, 2 * pair + 1]], axis=1)
                for q in range(4)
            ],
            axis=0,
        )
        across = dot_n(inverse_parts, right3(across, axis=0))
        change = dot_n(solved_parts, right3(across, axis=0))
        for half in range(2):
            k = 2 * pair + half
            value = front[k] - change[:, half * BLK : (half + 1) * BLK]
            out[pl.ds(k, PIVOTS, 8), :] = jnp.where(in_panel, 0.0, value)

    for i in range(4):

        @pl.when(group == i)
        def _():
            out[pl.ds(0, PIVOTS, 8), :] = solved[:, i * BLK : (i + 1) * BLK]

            @pl.when(leaf < 4)
            def _():
                rows = pl.ds(pl.multiple_of((leaf & 3) * BLK, BLK), BLK)
                out[pl.ds(0, BLK, 8), :] = l_ref[rows, i * BLK : (i + 1) * BLK]


def finish(place, front, columns, rows, factor, inverse):
    return pl.pallas_call(
        trailing_kernel,
        out_shape=jax.ShapeDtypeStruct((8 * PIVOTS, BLK), F32),
        in_specs=[pl.BlockSpec(memory_space=SMEM)] + [pl.BlockSpec(memory_space=VMEM)] * 9,
        out_specs=pl.BlockSpec(memory_space=VMEM),
        scratch_shapes=[VMEM((4, PIVOTS, BLK), F32), VMEM((4, 8, BLK, BLK), F32)],
        compiler_params=pltpu.CompilerParams(vmem_limit_bytes=28 * 2**20),
        cost_estimate=pl.CostEstimate(
            flops=5 * 10**9, bytes_accessed=12 * 2**20, transcendentals=0
        ),
    )(place, front, *columns, *rows, factor, inverse)


def group_swap(x, mask, sources=GROUPS):
    return lax.ppermute(x, GROUP, [(a, a ^ mask) for a in range(sources)])


def leaf_column(x, leaf):
    sent = [lax.ppermute(x, "leaf", [(y, 4 * to + y) for y in range(4)]) for to in (1, 2, 3)]
    return jnp.where(leaf < 4, x, sent[0] + sent[1] + sent[2])


def leaf_row(x):
    turned = [
        lax.ppermute(x, "leaf", [(a, (a & 12) | ((a + by) & 3)) for a in range(LEAVES)])
        for by in (1, 2, 3)
    ]
    return [x] + turned


def panel_columns(x, group):
    have = jnp.where(group < 4, x, group_swap(x, 5, 4))
    both = jnp.stack([have, group_swap(have, 1)])
    return both, group_swap(both, 2)


def behind(x, earlier):
    return lax.optimization_barrier((x, earlier))[0]


def local(pivot_block, coupling, parent_front, child_map):
    leaf = lax.axis_index("leaf")
    group = lax.axis_index(GROUP)
    place = jnp.stack([leaf, group]).astype(jnp.int32)
    coupled = coupling[0]
    near, across, far = [group_swap(coupled, mask) for mask in (1, 5, 4)]
    factor, factor_own, below, inverses = factor_child(place, pivot_block[0], coupled)
    near, across = solve_rows(factor, inverses, [near, across])
    (far,) = solve_rows(factor, inverses, [far])
    have = {0: below, 1: near, 5: across, 4: far}
    have.update({mask ^ 2: group_swap(x, 2) for mask, x in list(have.items())})
    products = update_blocks(place, child_map, [have[s] for s in range(GROUPS)])
    got = lax.all_to_all(products, "leaf", split_axis=0, concat_axis=0, tiled=True)
    front, column, above, corner = assemble(
        place, child_map, got, parent_front.reshape(8 * PIVOTS, BLK)
    )
    corner = leaf_column(corner, leaf)
    above = leaf_column(behind(above, corner), leaf)
    corner = jnp.concatenate(leaf_row(corner), axis=0)
    corners = panel_columns(corner, group)
    columns = panel_columns(behind(column, corners[0]), group)
    rows = leaf_row(above)
    panel_factor, panel_inverse = factor_panel(place, corners)
    result = finish(place, front, columns, rows, panel_factor, panel_inverse)
    return (
        factor_own[None],
        below[None],
        result.reshape(4, 1, BLK, 8, 1, BLK),
    )


def solution(mesh):
    return jax.shard_map(
        local,
        mesh=mesh,
        in_specs=(
            P("leaf", None, None),
            P("leaf", GROUP, None),
            P(None, "leaf", None, None, GROUP, None),
            P(),
        ),
        out_specs=(
            P("leaf", GROUP, None),
            P("leaf", GROUP, None),
            P(None, "leaf", None, None, GROUP, None),
        ),
        check_vma=False,
    )
```

```python
import functools

import jax
import jax.numpy as jnp
from jax import lax
from jax.experimental import pallas as pl
from jax.experimental.pallas import tpu as pltpu
from jax.sharding import PartitionSpec as P

F32 = jnp.float32
BF16 = jnp.bfloat16
S = 2048
BLK = 128
PIVOTS = 512
LEAVES = 16
GROUPS = 8
NB = 256
HB = 128
SUB = 32
STEPS = S // NB
VMEM = pltpu.VMEM
SMEM = pltpu.SMEM
GROUP = ("row", "col")


def dot_t(a, b):
    return lax.dot_general(a, b, (((1,), (1,)), ((), ())), preferred_element_type=F32)


def dot_n(a, b):
    return lax.dot_general(a, b, (((1,), (0,)), ((), ())), preferred_element_type=F32)


def halves(x):
    high = x.astype(BF16)
    low = (x - high.astype(F32)).astype(BF16)
    return high, low


def left3(x, axis=1):
    high, low = halves(x)
    return jnp.concatenate([high, high, low], axis=axis)


def right3(x, axis=1):
    high, low = halves(x)
    return jnp.concatenate([high, low, high], axis=axis)


def mul_t(a, b):
    return dot_t(left3(a), right3(b))


def mul_n(a, b):
    return dot_n(left3(a), right3(b, axis=0))


def eliminate(rows, base):
    groups = SUB // 8
    sub = lax.broadcasted_iota(jnp.int32, (8, HB), 0)
    state = [
        [rows[8 * a : 8 * a + 8, HB * h : HB * h + HB] for h in range(2)] for a in range(groups)
    ]
    cols = [
        [
            jnp.broadcast_to(rows[8 * a : 8 * a + 8, base + j : base + j + 1], (8, HB))
            if a >= j // 8
            else None
            for a in range(groups)
        ]
        for j in range(SUB)
    ]
    for k in range(SUB):
        own, line = divmod(k, 8)
        inv = lax.rsqrt(jnp.broadcast_to(cols[k][own][line : line + 1, :], (8, HB)))
        scaled = [cols[k][a] * inv if a >= own else None for a in range(groups)]
        below = list(scaled)
        below[own] = jnp.where(sub > line, scaled[own], 0.0)
        for j in range(k + 1, SUB):
            at, spot = divmod(j, 8)
            across = jnp.broadcast_to(scaled[at][spot : spot + 1, :], (8, HB))
            for a in range(at, groups):
                cols[j][a] = cols[j][a] - below[a] * across
        for h in range(2):
            pivot_row = jnp.broadcast_to(state[own][h][line : line + 1, :], (8, HB)) * inv
            state[own][h] = jnp.where(
                sub == line, pivot_row, state[own][h] - below[own] * pivot_row
            )
            for a in range(own + 1, groups):
                state[a][h] = state[a][h] - below[a] * pivot_row
    return jnp.concatenate([jnp.concatenate(pair, axis=1) for pair in state], axis=0)


def diag_small(block, work):
    row = lax.broadcasted_iota(jnp.int32, (HB, HB), 0)
    col = lax.broadcasted_iota(jnp.int32, (HB, HB), 1)
    work[:, :HB] = block
    work[:, HB:] = jnp.where(row == col, 1.0, 0.0)
    for base in range(0, HB, SUB):
        rows = eliminate(work[base : base + SUB, :], base)
        work[base : base + SUB, :] = rows
        after = base + SUB
        if after < HB:
            high = rows.astype(BF16).astype(F32)
            low = rows - high
            left = jnp.concatenate([high[:, :HB], high[:, :HB], low[:, :HB]], axis=0).astype(BF16)
            right = jnp.concatenate([high, low, high], axis=0).astype(BF16)
            product = lax.dot_general(
                left, right, (((0,), (0,)), ((), ())), preferred_element_type=F32
            )
            work[after:, :] = work[after:, :] - product[after:, :]
    return jnp.where(col >= row, work[:, :HB], 0.0), work[:, HB:]


def diag_block(block, work):
    upper_a, inv_a = diag_small(block[:HB, :HB], work)
    low_left = mul_t(block[HB:, :HB], inv_a)
    upper_b, inv_b = diag_small(block[HB:, HB:] - mul_t(low_left, low_left), work)
    inv_low = -mul_n(inv_b, mul_n(low_left, inv_a))
    zero = jnp.zeros((HB, HB), F32)
    factor = jnp.concatenate(
        [
            jnp.concatenate([upper_a.T, zero], axis=1),
            jnp.concatenate([low_left, upper_b.T], axis=1),
        ],
        axis=0,
    )
    inverse = jnp.concatenate(
        [
            jnp.concatenate([inv_a, zero], axis=1),
            jnp.concatenate([inv_low, inv_b], axis=1),
        ],
        axis=0,
    )
    return factor, inverse


def column_place(group, i, j):
    return (group & 3) ^ (2 * i + j) ^ (group >> 2)


def part(i):
    return pl.ds(pl.multiple_of(i * NB, NB), NB)


OWN = STEPS
TALL = 4
TALL_PANEL = 4
ROWS = (OWN + max(TALL, TALL_PANEL)) * NB


def tall(i, count):
    return pl.ds(pl.multiple_of(i * NB, NB), count * NB)


def factor_kernel(
    place, p_hbm, c_hbm, l_hbm, own_hbm, b_hbm, inv_ref, p_vmem, full, work, left, right, sems
):
    def p_copy(i):
        where = (pl.ds(i * NB, NB), pl.ds(0, (i + 1) * NB))
        return pltpu.make_async_copy(p_hbm.at[where], p_vmem.at[where], sems.at[i])

    def l_copy(j):
        where = (pl.ds(j * NB, S - j * NB), pl.ds(j * NB, NB))
        return pltpu.make_async_copy(full.at[where], l_hbm.at[where], sems.at[STEPS + 1 + j])

    c_copy = pltpu.make_async_copy(c_hbm, full.at[pl.ds(S, NB), :], sems.at[STEPS])
    def b_copy(j):
        cols = pl.ds(j * NB, NB)
        return pltpu.make_async_copy(
            full.at[pl.ds(S, NB), cols], b_hbm.at[:, cols], sems.at[2 * STEPS + 1 + j]
        )

    own_copy = pltpu.make_async_copy(
        full.at[part(place[1]), :], own_hbm, sems.at[3 * STEPS + 1]
    )
    for i in range(STEPS):
        p_copy(i).start()
    c_copy.start()

    def load_row(i):
        p_copy(i).wait()
        rows = slice(i * NB, (i + 1) * NB)
        for k in range(i + 1):
            cols = slice(k * NB, (k + 1) * NB)
            full[rows, cols] = p_vmem[rows, cols].astype(F32)
        if i + 1 < STEPS:
            full[rows, (i + 1) * NB :] = jnp.zeros((NB, S - (i + 1) * NB), F32)

    load_row(0)

    def step(j, _):
        factor, inverse = diag_block(full[part(j), part(j)], work)
        full[part(j), part(j)] = factor
        inv_ref[j] = inverse
        inverse_parts = right3(inverse)

        @pl.when(j == 0)
        def _():
            for i in range(1, STEPS):
                load_row(i)
            c_copy.wait()

        def panel(t, _):
            rows = tall(j + 1 + t * TALL_PANEL, TALL_PANEL)
            x = dot_t(left3(full[rows, part(j)]), inverse_parts)
            full[rows, part(j)] = x
            left[rows, :] = left3(x)
            right[rows, :] = right3(x)
            return 0

        lax.fori_loop(0, (OWN - j + TALL_PANEL - 1) // TALL_PANEL, panel, 0)
        for i in range(STEPS):

            @pl.when(j == i)
            def _():
                l_copy(i).start()
                b_copy(i).start()

        @pl.when(j == place[1])
        def _():
            own_copy.start()

        def trail(k, _):
            def trail_rows(t, _):
                rows = tall(k + t * TALL, TALL)
                full[rows, part(k)] = full[rows, part(k)] - dot_t(left[rows, :], right[part(k), :])
                return 0

            lax.fori_loop(0, (OWN + 1 - k + TALL - 1) // TALL, trail_rows, 0)
            return 0

        lax.fori_loop(j + 1, STEPS, trail, 0)
        return 0

    lax.fori_loop(0, STEPS, step, 0)
    for j in range(STEPS):
        l_copy(j).wait()
        b_copy(j).wait()
    own_copy.wait()


def factor_child(place, pivot, coupling):
    return pl.pallas_call(
        factor_kernel,
        out_shape=(
            jax.ShapeDtypeStruct((S, S), F32),
            jax.ShapeDtypeStruct((NB, S), F32),
            jax.ShapeDtypeStruct((NB, S), F32),
            jax.ShapeDtypeStruct((STEPS, NB, NB), F32),
        ),
        in_specs=[pl.BlockSpec(memory_space=SMEM)] + [pl.BlockSpec(memory_space=pl.ANY)] * 2,
        out_specs=(pl.BlockSpec(memory_space=pl.ANY),) * 3 + (pl.BlockSpec(memory_space=VMEM),),
        scratch_shapes=[
            VMEM((S, S), BF16),
            VMEM((ROWS, S), F32),
            VMEM((HB, 2 * HB), F32),
            VMEM((ROWS, 3 * NB), BF16),
            VMEM((ROWS, 3 * NB), BF16),
            pltpu.SemaphoreType.DMA((3 * STEPS + 2,)),
        ],
        compiler_params=pltpu.CompilerParams(vmem_limit_bytes=52 * 2**20),
        cost_estimate=pl.CostEstimate(
            flops=100 * 10**9, bytes_accessed=30 * 2**20, transcendentals=0
        ),
    )(place, pivot, coupling)


def solve_kernel(count, after, l_hbm, inv_ref, *refs):
    ins = refs[:count]
    outs = refs[count + after : 2 * count + after]
    l_vmem, c_vmem, parts, sems = refs[2 * count + after :]

    def l_copy(j):
        where = (pl.ds(j * NB, NB), pl.ds(0, (j + 1) * NB))
        return pltpu.make_async_copy(l_hbm.at[where], l_vmem.at[where], sems.at[j])

    def c_copy(j, i):
        cols = pl.ds(j * NB, NB)
        return pltpu.make_async_copy(
            ins[i].at[:, cols], c_vmem.at[pl.ds(i * NB, NB), cols], sems.at[STEPS + j * count + i]
        )

    for j in range(STEPS):
        l_copy(j).start()
        for i in range(count):
            c_copy(j, i).start()
    for j in range(STEPS):
        l_copy(j).wait()
        for i in range(count):
            c_copy(j, i).wait()
        rhs = c_vmem[:, j * NB : (j + 1) * NB]
        if j:
            strip = jnp.concatenate(
                [
                    right3(l_vmem[j * NB : (j + 1) * NB, k * NB : (k + 1) * NB])
                    for k in range(j)
                ],
                axis=1,
            )
            newest = 3 * (j - 1) * NB
            if newest:
                rhs = rhs - dot_t(parts[:, :newest], strip[:, :newest])
            rhs = rhs - dot_t(parts[:, newest : newest + 3 * NB], strip[:, newest:])
        x = mul_t(rhs, inv_ref[j])
        if j + 1 < STEPS:
            parts[:, 3 * j * NB : 3 * (j + 1) * NB] = left3(x)
        for i in range(count):
            outs[i][:, j * NB : (j + 1) * NB] = x[i * NB : (i + 1) * NB]


def solve_rows(factor, inverses, rows, after=()):
    count = len(rows)
    return pl.pallas_call(
        functools.partial(solve_kernel, count, len(after)),
        out_shape=(jax.ShapeDtypeStruct((NB, S), F32),) * count,
        in_specs=[pl.BlockSpec(memory_space=pl.ANY), pl.BlockSpec(memory_space=VMEM)]
        + [pl.BlockSpec(memory_space=pl.ANY)] * (count + len(after)),
        out_specs=(pl.BlockSpec(memory_space=VMEM),) * count,
        scratch_shapes=[
            VMEM((S, S), F32),
            VMEM((count * NB, S), F32),
            VMEM((count * NB, 3 * (S - NB)), BF16),
            pltpu.SemaphoreType.DMA((STEPS * (1 + count),)),
        ],
        compiler_params=pltpu.CompilerParams(vmem_limit_bytes=(24 + 10 * count) * 2**20),
        cost_estimate=pl.CostEstimate(
            flops=count * 7 * 10**9, bytes_accessed=24 * 2**20, transcendentals=0
        ),
    )(factor, inverses, *rows, *after)


def update_kernel(place, map_ref, *refs):
    ins = refs[:GROUPS]
    out, tiles, chosen, high, low, sems = refs[GROUPS:]
    leaf = place[0]
    group = place[1]
    for s in range(GROUPS):
        for half in range(2):
            tile = (group ^ s) * 2 + half
            dest = lax.rem(map_ref[leaf, tile], LEAVES)
            rows = pl.ds(half * BLK, BLK)
            pltpu.make_async_copy(ins[s].at[rows, :], tiles.at[dest], sems.at[dest]).start()
            for pick in range(2):

                @pl.when(dest == group + pick * GROUPS)
                def _():
                    pltpu.make_async_copy(
                        ins[s].at[rows, :],
                        chosen.at[pl.ds(pick * BLK, BLK), :],
                        sems.at[LEAVES + pick],
                    ).start()

    for pick in range(2):
        pltpu.make_async_copy(
            ins[0].at[pl.ds(0, BLK), :],
            chosen.at[pl.ds(pick * BLK, BLK), :],
            sems.at[LEAVES + pick],
        ).wait()
    high[...], low[...] = halves(chosen[...])
    together = 4

    def tile_group(q, _):
        for t in range(together):
            pltpu.make_async_copy(
                ins[0].at[pl.ds(0, BLK), :],
                tiles.at[q * together + t],
                sems.at[q * together + t],
            ).wait()
        rows = tiles[pl.ds(q * together, together)].reshape(together * BLK, S)
        r_high, r_low = halves(rows)
        product = (
            dot_t(r_high, high[...]) + dot_t(r_high, low[...]) + dot_t(r_low, high[...])
        )
        for t in range(together):
            for pick in range(2):
                out[q * together + t, pick] = product[
                    t * BLK : (t + 1) * BLK, pick * BLK : (pick + 1) * BLK
                ]
        return 0

    lax.fori_loop(0, LEAVES // together, tile_group, 0)


def update_blocks(place, child_map, rows):
    return pl.pallas_call(
        update_kernel,
        out_shape=jax.ShapeDtypeStruct((LEAVES, 2, BLK, BLK), F32),
        in_specs=[pl.BlockSpec(memory_space=SMEM)] * 2
        + [pl.BlockSpec(memory_space=pl.ANY)] * GROUPS,
        out_specs=pl.BlockSpec(memory_space=VMEM),
        scratch_shapes=[
            VMEM((LEAVES, BLK, S), F32),
            VMEM((2 * BLK, S), F32),
            VMEM((2 * BLK, S), BF16),
            VMEM((2 * BLK, S), BF16),
            pltpu.SemaphoreType.DMA((LEAVES + 2,)),
        ],
        compiler_params=pltpu.CompilerParams(vmem_limit_bytes=33 * 2**20),
        cost_estimate=pl.CostEstimate(
            flops=8 * 10**9, bytes_accessed=20 * 2**20, transcendentals=0
        ),
    )(place, child_map, *rows)


def assemble_kernel(
    place, map_ref, got, parent, front, column, above, corner, row_level, col_slot
):
    leaf = place[0]
    group = place[1]

    def find(c, _):
        level = jnp.int32(0)
        slots = [jnp.int32(0), jnp.int32(0)]
        for t in range(LEAVES):
            block = map_ref[c, t]
            residue = block & (LEAVES - 1)
            level = jnp.where(residue == leaf, block >> 4, level)
            for pick in range(2):
                slots[pick] = jnp.where(
                    residue == group + pick * GROUPS, block >> 3, slots[pick]
                )
        row_level[c] = level
        for pick in range(2):
            col_slot[c, pick] = slots[pick]
        return 0

    lax.fori_loop(0, LEAVES, find, 0)
    for k in range(8):
        front[k] = parent[pl.ds(k, 4 * BLK, 8), :]

    def subtract(c, _):
        rows = pl.ds(pl.multiple_of(row_level[c] * BLK, BLK), BLK)
        for pick in range(2):
            slot = col_slot[c, pick]
            front[slot, rows, :] = front[slot, rows, :] - got[c, pick]
        return 0

    lax.fori_loop(0, LEAVES, subtract, 0)
    column[...] = front[0]
    above[...] = front[:, :BLK, :]
    corner[...] = front[0, :BLK, :]


def assemble(place, child_map, got, parent):
    return pl.pallas_call(
        assemble_kernel,
        out_shape=(
            jax.ShapeDtypeStruct((8, 4 * BLK, BLK), F32),
            jax.ShapeDtypeStruct((4 * BLK, BLK), F32),
            jax.ShapeDtypeStruct((8, BLK, BLK), F32),
            jax.ShapeDtypeStruct((BLK, BLK), F32),
        ),
        in_specs=[pl.BlockSpec(memory_space=SMEM)] * 2 + [pl.BlockSpec(memory_space=VMEM)] * 2,
        out_specs=(pl.BlockSpec(memory_space=VMEM),) * 4,
        scratch_shapes=[SMEM((LEAVES,), jnp.int32), SMEM((LEAVES, 2), jnp.int32)],
        compiler_params=pltpu.CompilerParams(vmem_limit_bytes=16 * 2**20),
        cost_estimate=pl.CostEstimate(
            flops=10**6, bytes_accessed=6 * 2**20, transcendentals=0
        ),
    )(place, child_map, got, parent)


def panel_kernel(place, here, there, l_ref, inv_ref, block, work):
    leaf = place[0]
    group = place[1]
    for i, ref in enumerate((here, there)):
        for j in range(2):
            for q in range(4):
                rows = pl.ds(pl.multiple_of(((leaf - q) & 3) * BLK, BLK), BLK)
                block[column_place(group, i, j), rows, :] = ref[j, q * BLK : (q + 1) * BLK]

    def square(r, c):
        rows = slice(r * NB, (r + 1) * NB)
        return jnp.concatenate([block[2 * c, rows, :], block[2 * c + 1, rows, :]], axis=1)

    factor_a, inv_a = diag_block(square(0, 0), work)
    low_left = mul_t(square(1, 0), inv_a)
    factor_b, inv_b = diag_block(square(1, 1) - mul_t(low_left, low_left), work)
    zero = jnp.zeros((NB, NB), F32)
    l_ref[:NB, :NB] = factor_a
    l_ref[:NB, NB:] = zero
    l_ref[NB:, :NB] = low_left
    l_ref[NB:, NB:] = factor_b
    inv_ref[:NB, :NB] = inv_a
    inv_ref[:NB, NB:] = zero
    inv_ref[NB:, :NB] = -mul_n(inv_b, mul_n(low_left, inv_a))
    inv_ref[NB:, NB:] = inv_b


def factor_panel(place, columns):
    return pl.pallas_call(
        panel_kernel,
        out_shape=(jax.ShapeDtypeStruct((PIVOTS, PIVOTS), F32),) * 2,
        in_specs=[pl.BlockSpec(memory_space=SMEM)] + [pl.BlockSpec(memory_space=VMEM)] * 2,
        out_specs=(pl.BlockSpec(memory_space=VMEM),) * 2,
        scratch_shapes=[VMEM((4, PIVOTS, BLK), F32), VMEM((HB, 2 * HB), F32)],
        compiler_params=pltpu.CompilerParams(vmem_limit_bytes=16 * 2**20),
        cost_estimate=pl.CostEstimate(
            flops=25 * 10**9, bytes_accessed=4 * 2**20, transcendentals=0
        ),
    )(place, *columns)


def trailing_kernel(
    place, front, here, there, y0, y1, y2, y3, l_ref, inv_ref, out, panel, above
):
    leaf = place[0]
    group = place[1]
    for i, ref in enumerate((here, there)):
        for j in range(2):
            panel[column_place(group, i, j)] = ref[j]
    for i, ref in enumerate((y0, y1, y2, y3)):
        above[(leaf - i) & 3] = ref[...]
    inverse = inv_ref[...]
    own = jnp.concatenate([panel[i] for i in range(4)], axis=1)
    solved = mul_t(own, inverse)
    solved_parts = left3(solved)
    inverse_parts = left3(inverse)
    row = lax.broadcasted_iota(jnp.int32, (PIVOTS, BLK), 0)
    in_panel = (row < BLK) & (leaf < 4)
    for pair in range(4):
        across = jnp.concatenate(
            [
                jnp.concatenate([above[q, 2 * pair], above[q, 2 * pair + 1]], axis=1)
                for q in range(4)
            ],
            axis=0,
        )
        across = dot_n(inverse_parts, right3(across, axis=0))
        change = dot_n(solved_parts, right3(across, axis=0))
        for half in range(2):
            k = 2 * pair + half
            value = front[k] - change[:, half * BLK : (half + 1) * BLK]
            out[pl.ds(k, PIVOTS, 8), :] = jnp.where(in_panel, 0.0, value)

    for i in range(4):

        @pl.when(group == i)
        def _():
            out[pl.ds(0, PIVOTS, 8), :] = solved[:, i * BLK : (i + 1) * BLK]

            @pl.when(leaf < 4)
            def _():
                rows = pl.ds(pl.multiple_of((leaf & 3) * BLK, BLK), BLK)
                out[pl.ds(0, BLK, 8), :] = l_ref[rows, i * BLK : (i + 1) * BLK]


def finish(place, front, columns, rows, factor, inverse):
    return pl.pallas_call(
        trailing_kernel,
        out_shape=jax.ShapeDtypeStruct((8 * PIVOTS, BLK), F32),
        in_specs=[pl.BlockSpec(memory_space=SMEM)] + [pl.BlockSpec(memory_space=VMEM)] * 9,
        out_specs=pl.BlockSpec(memory_space=VMEM),
        scratch_shapes=[VMEM((4, PIVOTS, BLK), F32), VMEM((4, 8, BLK, BLK), F32)],
        compiler_params=pltpu.CompilerParams(vmem_limit_bytes=28 * 2**20),
        cost_estimate=pl.CostEstimate(
            flops=5 * 10**9, bytes_accessed=12 * 2**20, transcendentals=0
        ),
    )(place, front, *columns, *rows, factor, inverse)


def group_swap(x, mask, sources=GROUPS):
    return lax.ppermute(x, GROUP, [(a, a ^ mask) for a in range(sources)])


def leaf_column(x, leaf):
    sent = [lax.ppermute(x, "leaf", [(y, 4 * to + y) for y in range(4)]) for to in (1, 2, 3)]
    return jnp.where(leaf < 4, x, sent[0] + sent[1] + sent[2])


def leaf_row(x):
    turned = [
        lax.ppermute(x, "leaf", [(a, (a & 12) | ((a + by) & 3)) for a in range(LEAVES)])
        for by in (1, 2, 3)
    ]
    return [x] + turned


def panel_columns(x, group):
    have = jnp.where(group < 4, x, group_swap(x, 5, 4))
    both = jnp.stack([have, group_swap(have, 1)])
    return both, group_swap(both, 2)


def behind(x, earlier):
    return lax.optimization_barrier((x, earlier))[0]


def local(pivot_block, coupling, parent_front, child_map):
    leaf = lax.axis_index("leaf")
    group = lax.axis_index(GROUP)
    place = jnp.stack([leaf, group]).astype(jnp.int32)
    coupled = coupling[0]
    near, across, far = [group_swap(coupled, mask) for mask in (1, 5, 4)]
    factor, factor_own, below, inverses = factor_child(place, pivot_block[0], coupled)
    near, across = solve_rows(factor, inverses, [near, across])
    (far,) = solve_rows(factor, inverses, [far])
    have = {0: below, 1: near, 5: across, 4: far}
    have.update({mask ^ 2: group_swap(x, 2) for mask, x in list(have.items())})
    products = update_blocks(place, child_map, [have[s] for s in range(GROUPS)])
    got = lax.all_to_all(products, "leaf", split_axis=0, concat_axis=0, tiled=True)
    front, column, above, corner = assemble(
        place, child_map, got, parent_front.reshape(8 * PIVOTS, BLK)
    )
    corner = leaf_column(corner, leaf)
    above = leaf_column(behind(above, corner), leaf)
    corner = jnp.concatenate(leaf_row(corner), axis=0)
    columns = panel_columns(column, group)
    corners = panel_columns(behind(corner, columns[0]), group)
    rows = leaf_row(above)
    panel_factor, panel_inverse = factor_panel(place, corners)
    result = finish(place, front, columns, rows, panel_factor, panel_inverse)
    return (
        factor_own[None],
        below[None],
        result.reshape(4, 1, BLK, 8, 1, BLK),
    )


def solution(mesh):
    return jax.shard_map(
        local,
        mesh=mesh,
        in_specs=(
            P("leaf", None, None),
            P("leaf", GROUP, None),
            P(None, "leaf", None, None, GROUP, None),
            P(),
        ),
        out_specs=(
            P("leaf", GROUP, None),
            P("leaf", GROUP, None),
            P(None, "leaf", None, None, GROUP, None),
        ),
        check_vma=False,
    )
```
